512 devices in a mesh: grain: 64 (over x, z), plane: 8 (over y, core).
Axes of the slice: x: 4, y: 4, z: 16, core: 2. Of those that a mesh axis runs over, the one named last changes fastest.
Arguments:
- field: float32 [262144], P(('plane', 'grain')), may hold values from -16 to 16
- grain_positions: int32 [3, 16384], P(None, 'grain'), may hold values from -79 to 4095, as said below
- pixel_coords: int32 [3, 262144], P(None, 'plane'), may hold values from 0 to 4095, as said below
- block_grain: int32 [8, 2304], P('plane', 'grain'), may hold values from 0 to 3, as said below
- block_pixel: int32 [8, 2304], P('plane', 'grain'), may hold values from 0 to 127, as said below
- block_count: int32 [8, 64], P('plane', 'grain'), may hold values from 4 to 36, as said below
Outputs:
- moments: float32 [3, 16384], P(None, 'grain')
- residual: float32 [262144], P(('plane', 'grain'))
The draws below stay inside these ranges and needn't reach their ends.
Inputs may be any that keep to these rules, and one draw needn't show every extreme that they name: On each device, the first block_count slots name pairwise distinct pairs (block_grain, block_pixel); later slots hold valid indices and are ignored. `block_pixel`: paired with block_grain slot by slot. `block_count`: some device lists exactly 36 blocks. `grain_positions`: every grain's z is at most 0. `pixel_coords`: every pixel's z is at least 96.
All inputs are finite; a program needn't handle non-finite values.
Results may differ from the reference program's by a relative error of at most 0.0003.
Values sent between devices are 32-bit elements; how exact they have to be, the bound alone decides.
A program may use at most 64 MiB of HBM per device.

```python
import jax
import jax.numpy as jnp
from jax import lax

BLOCK_G = 64
BLOCK_P = 256
TILE_COLS = 8
ITERS = 3
GRAINS = 16384
PIXELS = 262144
GB_DEV = 4
PB_PL = 128
MAXB = 36
N_GRAIN = 64
N_PLANE = 8


tile_span = 256


pixel_pitch = 16


def grain_layout(key):
    grid_rows = PB_PL // TILE_COLS
    base = jax.random.fold_in(key, 23)
    shape = (N_GRAIN, GB_DEV)
    tile_col = jax.random.randint(jax.random.fold_in(base, 1), shape, 0, TILE_COLS)
    tile_row = jax.random.randint(jax.random.fold_in(base, 2), shape, 0, grid_rows)
    depth = jax.random.randint(jax.random.fold_in(base, 3), shape, 0, 5)
    forced = jax.random.randint(jax.random.fold_in(base, 4), (), 0, N_GRAIN)
    row_low = 1 if grid_rows >= 3 else 0
    row_high = grid_rows - 1 if grid_rows >= 3 else grid_rows
    inner_col = jax.random.randint(jax.random.fold_in(base, 5), shape, 1, TILE_COLS - 1)
    inner_row = jax.random.randint(jax.random.fold_in(base, 6), shape, row_low, row_high)
    chosen = lax.broadcasted_iota(jnp.int32, shape, 0) == forced
    tile_col = jnp.where(chosen, inner_col, tile_col)
    tile_row = jnp.where(chosen, inner_row, tile_row)
    depth = jnp.where(chosen, 4, depth)
    return (tile_col.astype(jnp.int32), tile_row.astype(jnp.int32), depth.astype(jnp.int32))


def pair_lists(key):
    tile_col, tile_row, depth = grain_layout(key)
    grid_rows = PB_PL // TILE_COLS
    level = jnp.arange(N_PLANE, dtype=jnp.int32) * 3 // (N_PLANE - 1)
    spread = depth[None, :, :] + level[:, None, None] >= 4
    reach_row = jnp.array([-1, -1, -1, 0, 0, 0, 1, 1, 1], jnp.int32)
    reach_col = jnp.array([-1, 0, 1, -1, 0, 1, -1, 0, 1], jnp.int32)
    centre = jnp.array([0, 0, 0, 0, 1, 0, 0, 0, 0], jnp.int32) == 1
    cand_row = tile_row[:, :, None] + reach_row
    cand_col = tile_col[:, :, None] + reach_col
    inside = (cand_row >= 0) & (cand_row < grid_rows) & (cand_col >= 0) & (cand_col < TILE_COLS)
    valid = inside[None] & (spread[..., None] | centre)
    flat_valid = valid.reshape(N_PLANE, N_GRAIN, GB_DEV * 9)
    tiles = (jnp.clip(cand_row, 0, grid_rows - 1) * TILE_COLS + jnp.clip(cand_col, 0, TILE_COLS - 1)).reshape(N_GRAIN, GB_DEV * 9)
    position = lax.broadcasted_iota(jnp.int32, flat_valid.shape, 2)
    score = jnp.where(flat_valid, 0, GB_DEV * 9) + position
    order = jnp.argsort(score, axis=-1, stable=True)[..., :MAXB].astype(jnp.int32)
    grain_part = order // 9
    pixel_part = jnp.take_along_axis(jnp.broadcast_to(tiles[None], flat_valid.shape), order, axis=-1)
    counts = jnp.sum(flat_valid.astype(jnp.int32), axis=-1)
    return (grain_part.reshape(N_PLANE, N_GRAIN * MAXB).astype(jnp.int32), pixel_part.reshape(N_PLANE, N_GRAIN * MAXB).astype(jnp.int32), counts.astype(jnp.int32))


def draw_block_grain(key, part):
    return pair_lists(key)[0]


def draw_block_pixel(key, part):
    return pair_lists(key)[1]


def draw_block_count(key, part):
    return pair_lists(key)[2]


def draw_grain_positions(key, part):
    tile_col, tile_row, depth = grain_layout(key)
    shape = (N_GRAIN, GB_DEV, BLOCK_G)
    across = jax.random.randint(jax.random.fold_in(key, 31), shape, 0, tile_span)
    along = jax.random.randint(jax.random.fold_in(key, 32), shape, 0, tile_span)
    below = jax.random.randint(jax.random.fold_in(key, 33), shape, 0, 16)
    coord_east = tile_col[..., None] * tile_span + across
    coord_north = tile_row[..., None] * tile_span + along
    coord_up = -16 * depth[..., None] - below
    return jnp.stack([coord_east, coord_north, coord_up]).reshape(3, GRAINS).astype(jnp.int32)


def draw_pixel_coords(key, part):
    shape = (N_PLANE, PB_PL, BLOCK_P)
    plane_index = lax.broadcasted_iota(jnp.int32, shape, 0)
    tile_index = lax.broadcasted_iota(jnp.int32, shape, 1)
    within = lax.broadcasted_iota(jnp.int32, shape, 2)
    jitter_east = jax.random.randint(jax.random.fold_in(key, 41), shape, 0, pixel_pitch)
    jitter_north = jax.random.randint(jax.random.fold_in(key, 42), shape, 0, pixel_pitch)
    lift = jax.random.randint(jax.random.fold_in(key, 43), shape, 0, 3)
    coord_east = tile_index % TILE_COLS * tile_span + within % 16 * pixel_pitch + jitter_east
    coord_north = tile_index // TILE_COLS * tile_span + within // 16 * pixel_pitch + jitter_north
    coord_up = 96 + 16 * plane_index + lift
    return jnp.stack([coord_east, coord_north, coord_up]).reshape(3, PIXELS).astype(jnp.int32)


def draw_field(key, part):
    blocks = PIXELS // BLOCK_P
    noise = jnp.clip(jax.random.normal(jax.random.fold_in(key, 1), (blocks, BLOCK_P), jnp.float32), -4.0, 4.0)
    scale = jnp.exp(jax.random.uniform(jax.random.fold_in(key, 2), (blocks, 1), jnp.float32) * 2.302585)
    return (0.4 * noise * scale).reshape(PIXELS).astype(jnp.float32)


def setup_inputs(seed: int = 0) -> dict:
    keys = jax.random.split(jax.random.key(seed), 7)
    field = draw_field(jax.random.fold_in(keys[6], 71), 0)
    grain_positions = draw_grain_positions(jax.random.fold_in(keys[6], 71), 0)
    pixel_coords = draw_pixel_coords(jax.random.fold_in(keys[6], 71), 0)
    block_grain = draw_block_grain(jax.random.fold_in(keys[6], 71), 0)
    block_pixel = draw_block_pixel(jax.random.fold_in(keys[6], 71), 0)
    block_count = draw_block_count(jax.random.fold_in(keys[6], 71), 0)
    return {"field": field, "grain_positions": grain_positions, "pixel_coords": pixel_coords, "block_grain": block_grain, "block_pixel": block_pixel, "block_count": block_count}


field_scale = 27.0
grid_step = 0.03125

def sensitivities(grain_xyz, pixel_xyz):
    diff = pixel_xyz[:, :, None, :] - grain_xyz[:, :, :, None]
    dist_sq = lax.optimization_barrier(jnp.sum(diff * diff, axis=0))
    inverse = field_scale / (dist_sq * jnp.sqrt(dist_sq))
    along = 3.0 * diff[2] / dist_sq
    return jnp.stack([along * diff[0] * inverse, along * diff[1] * inverse, (along * diff[2] - 1.0) * inverse])

def reference(field, grain_positions, pixel_coords, block_grain, block_pixel, block_count):
    grain_xyz = (grain_positions.astype(jnp.float32) * grid_step).reshape(3, -1, BLOCK_G)
    pixel_xyz = (pixel_coords.astype(jnp.float32) * grid_step).reshape(3, -1, BLOCK_P)
    grain_total = grain_xyz.shape[1]
    pixel_total = pixel_xyz.shape[1]
    slot = jnp.arange(MAXB, dtype=jnp.int32)
    grain_base = (jnp.arange(N_GRAIN, dtype=jnp.int32) * GB_DEV)[None, :, None]
    pixel_base = (jnp.arange(N_PLANE, dtype=jnp.int32) * PB_PL)[:, None, None]
    grain_ids = (block_grain.reshape(N_PLANE, N_GRAIN, MAXB) + grain_base).astype(jnp.int32).reshape(-1, MAXB)
    pixel_ids = (block_pixel.reshape(N_PLANE, N_GRAIN, MAXB) + pixel_base).astype(jnp.int32).reshape(-1, MAXB)
    weights = (slot[None, None, :] < block_count[:, :, None]).astype(jnp.float32).reshape(-1, MAXB)
    highest = lax.Precision.HIGHEST

    def forward(moment_blocks):

        def step(acc, group):
            gidx, pidx, weight = group
            kern = sensitivities(grain_xyz[:, gidx], pixel_xyz[:, pidx])
            contrib = jnp.einsum('cbgp,cbg->bp', kern, moment_blocks[:, gidx], precision=highest) * weight[:, None]
            return (acc.at[pidx].add(contrib), None)
        acc, ignored = lax.scan(step, jnp.zeros((pixel_total, BLOCK_P), jnp.float32), (grain_ids, pixel_ids, weights))
        return acc.reshape(-1)

    def backward(values):
        rows = values.reshape(pixel_total, BLOCK_P)

        def step(acc, group):
            gidx, pidx, weight = group
            kern = sensitivities(grain_xyz[:, gidx], pixel_xyz[:, pidx])
            contrib = jnp.einsum('cbgp,bp->cbg', kern, rows[pidx] * weight[:, None], precision=highest)
            return (acc.at[:, gidx].add(contrib), None)
        acc, ignored = lax.scan(step, jnp.zeros((3, grain_total, BLOCK_G), jnp.float32), (grain_ids, pixel_ids, weights))
        return acc
    moments = jnp.zeros((3, grain_total, BLOCK_G), jnp.float32)
    residual = field
    grad = backward(residual)
    direction = grad
    gamma = jnp.sum(grad * grad)
    for step_index in range(ITERS):
        image = forward(direction)
        alpha = gamma / jnp.sum(image * image)
        moments = moments + alpha * direction
        residual = residual - alpha * image
        if step_index + 1 < ITERS:
            grad = backward(residual)
            gamma_next = jnp.sum(grad * grad)
            direction = grad + gamma_next / gamma * direction
            gamma = gamma_next
    return (moments.reshape(3, -1), residual)
```

```python
import functools

import jax
import jax.numpy as jnp
from jax import lax
from jax.experimental import pallas as pl
from jax.experimental.pallas import tpu as pltpu
from jax.sharding import PartitionSpec as P

MESH = pl.DeviceIdType.MESH
BLOCK_G = 64
ITERS = 3
SLOTS = 36
GROUPS = 8
F32 = jnp.float32


def tables(block_grain, block_pixel, block_count):
    slot = jnp.arange(SLOTS, dtype=jnp.int32)
    live = slot < block_count[0, 0]
    key = jnp.where(live, block_grain[0], 4)
    before = (key[None, :] < key[:, None]) | ((key[None, :] == key[:, None]) & (slot[None, :] < slot[:, None]))
    rank = jnp.sum(before.astype(jnp.int32), axis=1)
    place = (rank[None, :] == slot[:, None]).astype(jnp.int32)
    pixel = jnp.sum(place * block_pixel[0][None, :], axis=1)
    grain = jnp.minimum(jnp.sum(place * key[None, :], axis=1), 3)
    alive = jnp.sum(place * live.astype(jnp.int32)[None, :], axis=1)
    upto = jnp.sum((key[None, :] <= grain[:, None]).astype(jnp.int32), axis=1)
    below = jnp.sum((key[None, :] < grain[:, None]).astype(jnp.int32), axis=1)
    same = ((slot > below) | (alive == 0)).astype(jnp.int32)
    same = jnp.where((slot == 0), 0, same)
    each = jnp.arange(SLOTS, dtype=jnp.int32)
    last = jnp.maximum(jnp.sum((key[None, :] <= each[:, None]).astype(jnp.int32), axis=1) - 1, 0)
    held = (jnp.sum((key[None, :] == each[:, None]).astype(jnp.int32), axis=1) > 0).astype(jnp.int32)
    del upto
    table = jnp.stack([pixel, grain, alive, same, last, held])
    half = jnp.arange(2, dtype=jnp.int32)
    target = jnp.where(alive[:, None] > 0, 2 * pixel[:, None] + half[None, :], -1).reshape(1, 2 * SLOTS)
    target = jnp.concatenate([target, jnp.full((1, 128 - 2 * SLOTS), -1, jnp.int32)], axis=1)
    return table, target


def kernel(
    sizes,
    table,
    target,
    field,
    grains,
    pixels,
    moments_out,
    residual_out,
    coords,
    sens,
    spread,
    snap,
    picks,
    contrib,
    rows,
    gather_send,
    gathered,
    part_send,
    part_recv,
    grad_send,
    grad_recv,
    gamma_send,
    gamma_recv,
    norm_send,
    norm_recv,
    total_send,
    total_recv,
    gather_sem,
    part_sem,
    grad_sem,
    gamma_sem,
    last_sem,
):
    nx, nz, npl = sizes
    ng = nx * nz
    far = nz // 2
    g, p = lax.axis_index("grain"), lax.axis_index("plane")
    x, z = g // nz, lax.rem(g, nz)

    def grain_peer(i):
        m = i // nx
        a = lax.rem(i + 1, nx)
        d = far + (1 - 2 * lax.rem(m, 2)) * ((m + 1) // 2)
        return lax.rem(x + a, nx) * nz + lax.rem(z + d, nz)

    def plane_peer(i):
        return lax.rem(p + i + 1, npl)

    def each(n, body):
        def step(i, carry):
            body(i)
            return carry

        lax.fori_loop(0, n, step, 0)

    def to_grains(source, place, send_sem, recv_sem):
        def send(i):
            peer = grain_peer(i)
            pltpu.make_async_remote_copy(
                src_ref=source(peer),
                dst_ref=place(i),
                send_sem=send_sem,
                recv_sem=recv_sem,
                device_id=(peer, p),
                device_id_type=MESH,
            ).start()

        each(ng - 1, send)

    def to_planes(source, place, send_sem, recv_sem):
        def send(i):
            pltpu.make_async_remote_copy(
                src_ref=source,
                dst_ref=place(i),
                send_sem=send_sem,
                recv_sem=recv_sem,
                device_id=(g, plane_peer(i)),
                device_id_type=MESH,
            ).start()

        each(npl - 1, send)

    def wait(ref, sem):
        pltpu.make_async_copy(ref, ref, sem).wait()

    barrier = pltpu.get_barrier_semaphore()
    each(
        ng - 1,
        lambda i: pl.semaphore_signal(barrier, inc=1, device_id=(grain_peer(i), p), device_id_type=MESH),
    )
    each(
        npl - 1,
        lambda i: pl.semaphore_signal(barrier, inc=1, device_id=(g, plane_peer(i)), device_id_type=MESH),
    )

    lane = lax.broadcasted_iota(jnp.int32, (8, 128), 1)

    def broadcast_lanes(tile):
        for r in range(96):
            c, b, k = r // 32, r // 8 % 4, r % 8
            spread[b, c, k] = jnp.broadcast_to(tile[:, r : r + 1], (8, 128))

    broadcast_lanes(grains[...].astype(F32) * 0.03125)
    picks[...] = (lax.broadcasted_iota(jnp.int32, (4 * ng, 128), 0) == target[...]).astype(F32)
    contrib[...] = jnp.zeros((128, 128), F32)

    for c in range(3):
        coords[c] = (pixels[c : c + 1, :].astype(F32) * 0.03125).reshape(4 * ng, 128)

    def make_sens(j):
        e, b = table[0, j], table[1, j]
        scale = table[2, j].astype(F32) * 27.0
        for h in range(2):
            px, py, pz = (coords[c, pl.ds(2 * e + h, 1), :] for c in range(3))
            for k in range(GROUPS):
                dx = px - spread[b, 0, k]
                dy = py - spread[b, 1, k]
                dz = pz - spread[b, 2, k]
                inv = lax.rsqrt(dx * dx + dy * dy + dz * dz)
                inv2 = inv * inv
                inv3 = inv2 * inv * scale
                along = 3.0 * dz * inv2 * inv3
                sens[j, 0, k, h] = along * dx
                sens[j, 1, k, h] = along * dy
                sens[j, 2, k, h] = along * dz - inv3

    def gather(it):
        to_grains(lambda peer: gather_send.at[it], lambda i: gathered.at[it, g], gather_sem.at[0, it], gather_sem.at[1, it])
        gathered[it, g] = gather_send[it]

    def gather_wait(it):
        wait(gathered.at[it, pl.ds(0, ng - 1)], gather_sem.at[1, it])

    def backward():
        def step(j, acc):
            e = table[0, j]
            keep = table[3, j].astype(F32)
            v0 = jnp.broadcast_to(rows[pl.ds(2 * e, 1), :], (8, 128))
            v1 = jnp.broadcast_to(rows[pl.ds(2 * e + 1, 1), :], (8, 128))
            out = []
            for c in range(3):
                for k in range(GROUPS):
                    i = c * GROUPS + k
                    t = acc[i] * keep + (sens[j, c, k, 0] * v0 + sens[j, c, k, 1] * v1)
                    snap[j, i] = t
                    out.append(t)
            return tuple(out)

        lax.fori_loop(0, SLOTS, step, tuple(jnp.zeros((8, 128), F32) for _ in range(24)))
        total = jnp.zeros((8, 128), F32)
        for b in range(4):
            last = table[4, b]
            held = table[5, b].astype(F32)
            for i in range(24):
                s = jnp.sum(snap[last, i], axis=1, keepdims=True) * held
                total = jnp.where(lane == (i // 8) * 32 + b * 8 + i % 8, s, total)
        return total

    def forward(it):
        def step(j, carry):
            b = table[1, j]
            acc = [[jnp.zeros((8, 128), F32) for _ in range(2)] for _ in range(2)]
            for c in range(3):
                for k in range(GROUPS):
                    d = spread[b, c, k]
                    for h in range(2):
                        acc[h][k % 2] = acc[h][k % 2] + sens[j, c, k, h] * d
            for h in range(2):
                contrib[pl.ds(2 * j + h, 1), :] = jnp.sum(acc[h][0] + acc[h][1], axis=0, keepdims=True)
            return carry

        lax.fori_loop(0, SLOTS, step, 0)
        part = jnp.dot(picks[...], contrib[...], precision=lax.Precision.HIGHEST, preferred_element_type=F32)
        part_send[it] = part.reshape(ng, 4, 128)
        to_grains(lambda peer: part_send.at[it, peer], lambda i: part_recv.at[it, i], part_sem.at[0, it], part_sem.at[1, it])
        wait(part_recv.at[it], part_sem.at[1, it])
        return jnp.sum(part_recv[it], axis=0) + part_send[it, g]

    def plane_sum(it, tile):
        grad_send[it] = tile
        to_planes(grad_send.at[it], lambda i: grad_recv.at[it, i], grad_sem.at[0, it], grad_sem.at[1, it])
        wait(grad_recv.at[it], grad_sem.at[1, it])
        return tile + jnp.sum(grad_recv[it], axis=0)

    def full_sum(tile):
        return jnp.sum(jnp.sum(tile, axis=0, keepdims=True), axis=1, keepdims=True)

    gather_send[0] = field[...]
    pl.semaphore_wait(barrier, ng - 1 + npl - 1)
    gather(0)
    each(SLOTS, make_sens)
    gather_wait(0)
    rows[...] = gathered[0].reshape(4 * ng, 128)

    grad = plane_sum(0, backward())
    residual = field[...]
    moments = direction = jnp.zeros((8, 128), F32)
    image = jnp.zeros((4, 128), F32)
    gamma = jnp.ones((1, 1), F32)
    for it in range(ITERS):
        mine = full_sum(grad * grad)
        gamma_send[it] = jnp.broadcast_to(mine, (1, 128))
        to_grains(lambda peer: gamma_send.at[it], lambda i: gamma_recv.at[it, i], gamma_sem.at[0, it], gamma_sem.at[1, it])
        broadcast_lanes(grad)
        image_new = forward(it)
        wait(gamma_recv.at[it], gamma_sem.at[1, it])
        gamma_new = mine + jnp.sum(gamma_recv[it], axis=0)[:, 0:1]
        if it == 0:
            direction, image = grad, image_new
        else:
            beta = gamma_new / gamma
            direction = grad + beta * direction
            image = image_new + beta * image
        gamma = gamma_new
        if it + 1 < ITERS:
            gather_send[it + 1] = image
            gather(it + 1)
            gather_wait(it + 1)
            full = gathered[it + 1].reshape(4 * ng, 128)
            rows[...] = full
            tile = jnp.where(lane >= 96, full_sum(full * full), backward())
            tile = plane_sum(it + 1, tile)
            alpha = gamma / tile[0:1, 96:97]
            moments = moments + alpha * direction
            residual = residual - alpha * image
            grad = jnp.where(lane >= 96, 0.0, grad - alpha * tile)
        else:
            norm = full_sum(image * image)
            norm_send[...] = jnp.broadcast_to(norm, (1, 128))
            to_planes(norm_send, lambda i: norm_recv.at[i], last_sem.at[0], last_sem.at[1])
            wait(norm_recv, last_sem.at[1])
            over_planes = norm + jnp.sum(norm_recv[...], axis=0)[:, 0:1]
            total_send[...] = jnp.broadcast_to(over_planes, (1, 128))
            to_grains(lambda peer: total_send, lambda i: total_recv.at[i], last_sem.at[2], last_sem.at[3])
            wait(total_recv, last_sem.at[3])
            alpha = gamma / (over_planes + jnp.sum(total_recv[...], axis=0)[:, 0:1])
            moments_out[...] = moments + alpha * direction
            residual_out[...] = residual - alpha * image

    for it in range(ITERS):
        wait(gathered.at[it, pl.ds(0, ng - 1)], gather_sem.at[0, it])
        wait(part_recv.at[it], part_sem.at[0, it])
        wait(grad_recv.at[it], grad_sem.at[0, it])
        wait(gamma_recv.at[it], gamma_sem.at[0, it])
    wait(norm_recv, last_sem.at[0])
    wait(total_recv, last_sem.at[2])


def local(sizes, field, grain_positions, pixel_coords, block_grain, block_pixel, block_count):
    nx, nz, npl = sizes
    ng = nx * nz
    table, target = tables(block_grain, block_pixel, block_count)
    grains = grain_positions.reshape(3, 32, 8).transpose(2, 0, 1).reshape(8, 96)
    grains = jnp.concatenate([grains, jnp.zeros((8, 32), jnp.int32)], axis=1)
    vmem = pl.BlockSpec(memory_space=pltpu.VMEM)
    moments, residual = pl.pallas_call(
        functools.partial(kernel, sizes),
        out_shape=(jax.ShapeDtypeStruct((8, 128), F32), jax.ShapeDtypeStruct((4, 128), F32)),
        in_specs=[pl.BlockSpec(memory_space=pltpu.SMEM)] + [vmem] * 4,
        out_specs=(vmem, vmem),
        scratch_shapes=[
            pltpu.VMEM((3, 4 * ng, 128), F32),
            pltpu.VMEM((SLOTS, 3, GROUPS, 2, 8, 128), F32),
            pltpu.VMEM((4, 3, GROUPS, 8, 128), F32),
            pltpu.VMEM((SLOTS, 24, 8, 128), F32),
            pltpu.VMEM((4 * ng, 128), F32),
            pltpu.VMEM((128, 128), F32),
            pltpu.VMEM((4 * ng, 128), F32),
            pltpu.VMEM((ITERS, 4, 128), F32),
            pltpu.VMEM((ITERS, ng, 4, 128), F32),
            pltpu.VMEM((ITERS, ng, 4, 128), F32),
            pltpu.VMEM((ITERS, ng - 1, 4, 128), F32),
            pltpu.VMEM((ITERS, 8, 128), F32),
            pltpu.VMEM((ITERS, npl - 1, 8, 128), F32),
            pltpu.VMEM((ITERS, 1, 128), F32),
            pltpu.VMEM((ITERS, ng - 1, 1, 128), F32),
            pltpu.VMEM((1, 128), F32),
            pltpu.VMEM((npl - 1, 1, 128), F32),
            pltpu.VMEM((1, 128), F32),
            pltpu.VMEM((ng - 1, 1, 128), F32),
            pltpu.SemaphoreType.DMA((2, ITERS)),
            pltpu.SemaphoreType.DMA((2, ITERS)),
            pltpu.SemaphoreType.DMA((2, ITERS)),
            pltpu.SemaphoreType.DMA((2, ITERS)),
            pltpu.SemaphoreType.DMA((4,)),
        ],
        compiler_params=pltpu.CompilerParams(collective_id=1, has_side_effects=True, vmem_limit_bytes=40 << 20),
        name="solve",
    )(table, target, field.reshape(4, 128), grains, pixel_coords)
    moments = moments[:, :96].reshape(8, 3, 32).transpose(1, 2, 0).reshape(3, 256)
    return moments, residual.reshape(512)


def solution(mesh, rows=4):
    grain, plane = mesh.shape["grain"], mesh.shape["plane"]
    placed = (
        P(("plane", "grain")),
        P(None, "grain"),
        P(None, "plane"),
        P("plane", "grain"),
        P("plane", "grain"),
        P("plane", "grain"),
    )
    return jax.shard_map(
        functools.partial(local, (rows, grain // rows, plane)),
        mesh=mesh,
        in_specs=placed,
        out_specs=(P(None, "grain"), P(("plane", "grain"))),
        check_vma=False,
    )
```

```python
import functools

import jax
import jax.numpy as jnp
from jax import lax
from jax.experimental import pallas as pl
from jax.experimental.pallas import tpu as pltpu
from jax.sharding import PartitionSpec as P

MESH = pl.DeviceIdType.MESH
BLOCK_G = 64
ITERS = 3
SLOTS = 36
GROUPS = 8
F32 = jnp.float32


def kernel(
    sizes,
    field_in,
    grains_in,
    pixels_in,
    block_grain_in,
    block_pixel_in,
    block_count_in,
    moments_out,
    residual_out,
    field,
    grains,
    pixels,
    block_grain,
    block_pixel,
    block_count,
    table_made,
    table,
    coords,
    sens,
    spread,
    snap,
    picks,
    unfold,
    contrib,
    rows,
    gather_send,
    gathered,
    part_send,
    part_recv,
    grad_send,
    grad_recv,
    norm_send,
    norm_recv,
    total_send,
    total_recv,
    gather_sem,
    part_sem,
    grad_sem,
    last_sem,
    local_sem,
):
    nx, nz, npl = sizes
    ng = nx * nz
    far = nz // 2
    g, p = lax.axis_index("grain"), lax.axis_index("plane")
    x, z = g // nz, lax.rem(g, nz)

    columns = [lax.rem(x + a, nx) * nz for a in range(nx)]

    def grain_peers(body):
        def far_row(m, carry):
            d = far + (1 - 2 * lax.rem(m, 2)) * ((m + 1) // 2)
            row = lax.rem(z + d, nz)
            for a in range(nx):
                body(m * nx + a, columns[a] + row)
            return carry

        lax.fori_loop(0, nz - 1, far_row, 0)
        for a in range(1, nx):
            body((nz - 1) * nx + a - 1, columns[a] + z)

    def plane_peer(i):
        return lax.rem(p + i + 1, npl)

    def each(n, body):
        def step(i, carry):
            body(i)
            return carry

        lax.fori_loop(0, n, step, 0)

    def to_grains(source, place, send_sem, recv_sem):
        def send(i, peer):
            pltpu.make_async_remote_copy(
                src_ref=source(peer),
                dst_ref=place(i),
                send_sem=send_sem,
                recv_sem=recv_sem,
                device_id=(peer, p),
                device_id_type=MESH,
            ).start()

        grain_peers(send)

    def to_planes(source, place, send_sem, recv_sem):
        def send(i):
            pltpu.make_async_remote_copy(
                src_ref=source,
                dst_ref=place(i),
                send_sem=send_sem,
                recv_sem=recv_sem,
                device_id=(g, plane_peer(i)),
                device_id_type=MESH,
            ).start()

        each(npl - 1, send)

    def wait(ref, sem):
        pltpu.make_async_copy(ref, ref, sem).wait()

    barrier = pltpu.get_barrier_semaphore()
    loads = [
        pltpu.make_async_copy(src, dst, local_sem.at[i])
        for i, (src, dst) in enumerate(
            [
                (block_grain_in, block_grain),
                (block_pixel_in, block_pixel),
                (block_count_in, block_count),
                (grains_in, grains),
                (pixels_in, pixels),
                (field_in, field),
            ]
        )
    ]
    for load in loads:
        load.start()
    grain_peers(lambda i, peer: pl.semaphore_signal(barrier, inc=1, device_id=(peer, p), device_id_type=MESH))
    each(
        npl - 1,
        lambda i: pl.semaphore_signal(barrier, inc=1, device_id=(g, plane_peer(i)), device_id_type=MESH),
    )
    for load in loads:
        load.wait()

    lane = lax.broadcasted_iota(jnp.int32, (8, 128), 1)

    def broadcast_lanes(tile):
        for r in range(96):
            c, b, k = r // 32, r // 8 % 4, r % 8
            spread[b, c, k] = jnp.broadcast_to(tile[:, r : r + 1], (8, 128))

    sub, col = (lax.broadcasted_iota(jnp.int32, (40, 128), i) for i in range(2))
    slot = jnp.where(col < 64, col, col - 64)
    row = lax.broadcasted_iota(jnp.int32, (1, 128), 1)
    edge = lax.broadcasted_iota(jnp.int32, (1, SLOTS), 1)
    count = block_count[...]

    def wide(value, fill):
        return jnp.concatenate([value, jnp.full((1, 128 - SLOTS), fill, jnp.int32)], axis=1)

    def upright(value):
        return jnp.sum(jnp.where(sub == col, value, 0), axis=1, keepdims=True)

    def over_slots(value):
        return jnp.sum(value, axis=0, keepdims=True)

    key = wide(jnp.where(edge < count, block_grain[...], 4), 5)
    key_up = upright(key)
    real = sub[:, 0:1] < SLOTS
    ahead = (key < key_up) | ((key == key_up) & (col < sub))
    rank = jnp.sum(ahead.astype(jnp.int32), axis=1, keepdims=True)
    place = (rank == slot) & real
    pixel = over_slots(jnp.where(place, upright(wide(block_pixel[...], 0)), 0))
    block = over_slots(jnp.where(place, key_up, 0))
    alive = over_slots(jnp.where(place & (key_up < 4), 1, 0))
    block = jnp.minimum(block, 3)
    below = over_slots(jnp.where((key_up < block) & real, 1, 0))
    same = jnp.where((row > 0) & ((row > below) | (alive == 0)), 1, 0)
    upto = over_slots(jnp.where((key_up <= row) & real, 1, 0))
    held = over_slots(jnp.where((key_up == row) & real, 1, 0))
    zero = jnp.zeros((1, 128), jnp.int32)
    table_made[...] = jnp.concatenate(
        [pixel, block, alive, same, jnp.maximum(upto - 1, 0), jnp.minimum(held, 1), zero, zero], axis=0
    )
    to_scalars = pltpu.make_async_copy(table_made, table, local_sem.at[6])
    to_scalars.start()
    target = jnp.where(alive > 0, 2 * pixel + jnp.where(row < 64, 0, 1), -1)
    picks[...] = (lax.broadcasted_iota(jnp.int32, (4 * ng, 128), 0) == target).astype(F32)

    grain_s = lax.broadcasted_iota(jnp.int32, (8, 256), 0) == lax.rem(lax.broadcasted_iota(jnp.int32, (8, 256), 1), 8)

    def product(a, b, over):
        return lax.dot_general(
            a, b, (((1,), (over,)), ((), ())), precision=lax.Precision.HIGHEST, preferred_element_type=F32
        )

    for c in range(3):
        eighth = lax.broadcasted_iota(jnp.int32, (256, 128), 0) // 8
        unfold[c] = (eighth + 32 * c == lax.broadcasted_iota(jnp.int32, (256, 128), 1)).astype(F32)

    def to_tile(value):
        return sum(product(jnp.where(grain_s, value[c : c + 1, :], 0.0), unfold[c], 0) for c in range(3))

    def from_tile(tile):
        parts = [jnp.sum(jnp.where(grain_s, product(tile, unfold[c], 1), 0.0), axis=0, keepdims=True) for c in range(3)]
        return jnp.concatenate(parts, axis=0)

    broadcast_lanes(to_tile(grains[...].astype(F32) * 0.03125))
    contrib[...] = jnp.zeros((128, 128), F32)

    for c in range(3):
        coords[c] = (pixels[c : c + 1, :].astype(F32) * 0.03125).reshape(4 * ng, 128)

    def make_sens(j):
        e, b = table[0, j], table[1, j]
        scale = table[2, j].astype(F32) * 27.0
        for h in range(2):
            px, py, pz = (coords[c, pl.ds(2 * e + h, 1), :] for c in range(3))
            for k in range(GROUPS):
                dx = px - spread[b, 0, k]
                dy = py - spread[b, 1, k]
                dz = pz - spread[b, 2, k]
                inv = lax.rsqrt(dx * dx + dy * dy + dz * dz)
                inv2 = inv * inv
                inv3 = inv2 * inv * scale
                along = 3.0 * dz * inv2 * inv3
                sens[j, 0, k, h] = along * dx
                sens[j, 1, k, h] = along * dy
                sens[j, 2, k, h] = along * dz - inv3

    def gather(it):
        to_grains(lambda peer: gather_send.at[it], lambda i: gathered.at[it, g], gather_sem.at[0, it], gather_sem.at[1, it])
        gathered[it, g] = gather_send[it]

    def gather_wait(it):
        wait(gathered.at[it, pl.ds(0, ng - 1)], gather_sem.at[1, it])

    def backward():
        def step(j, acc):
            e = table[0, j]
            keep = table[3, j].astype(F32)
            v0 = jnp.broadcast_to(rows[pl.ds(2 * e, 1), :], (8, 128))
            v1 = jnp.broadcast_to(rows[pl.ds(2 * e + 1, 1), :], (8, 128))
            out = []
            for c in range(3):
                for k in range(GROUPS):
                    i = c * GROUPS + k
                    t = acc[i] * keep + (sens[j, c, k, 0] * v0 + sens[j, c, k, 1] * v1)
                    snap[j, i] = t
                    out.append(t)
            return tuple(out)

        lax.fori_loop(0, SLOTS, step, tuple(jnp.zeros((8, 128), F32) for _ in range(24)))
        total = jnp.zeros((8, 128), F32)
        for b in range(4):
            last = table[4, b]
            held = table[5, b].astype(F32)
            for i in range(24):
                s = jnp.sum(snap[last, i], axis=1, keepdims=True) * held
                total = jnp.where(lane == (i // 8) * 32 + b * 8 + i % 8, s, total)
        return total

    def forward(it):
        def step(j, carry):
            b = table[1, j]
            acc = [[jnp.zeros((8, 128), F32) for _ in range(2)] for _ in range(2)]
            for c in range(3):
                for k in range(GROUPS):
                    d = spread[b, c, k]
                    for h in range(2):
                        acc[h][k % 2] = acc[h][k % 2] + sens[j, c, k, h] * d
            for h in range(2):
                contrib[pl.ds(64 * h + j, 1), :] = jnp.sum(acc[h][0] + acc[h][1], axis=0, keepdims=True)
            return carry

        lax.fori_loop(0, SLOTS, step, 0)
        part = jnp.dot(picks[...], contrib[...], precision=lax.Precision.HIGHEST, preferred_element_type=F32)
        part_send[it] = part.reshape(ng, 4, 128)
        to_grains(lambda peer: part_send.at[it, peer], lambda i: part_recv.at[it, i], part_sem.at[0, it], part_sem.at[1, it])
        wait(part_recv.at[it], part_sem.at[1, it])
        return jnp.sum(part_recv[it], axis=0) + part_send[it, g]

    def plane_sum(it, tile):
        grad_send[it] = tile
        to_planes(grad_send.at[it], lambda i: grad_recv.at[it, i], grad_sem.at[0, it], grad_sem.at[1, it])
        wait(grad_recv.at[it], grad_sem.at[1, it])
        return tile + jnp.sum(grad_recv[it], axis=0)

    def full_sum(tile):
        folded = jnp.sum(tile.reshape(-1, 4, 128), axis=0)
        return jnp.sum(jnp.sum(folded, axis=0, keepdims=True), axis=1, keepdims=True)

    to_scalars.wait()
    pl.semaphore_wait(barrier, ng - 1 + npl - 1)
    gather_send[0] = field[...]
    gather(0)
    each(SLOTS, make_sens)
    gather_wait(0)
    full_residual = gathered[0].reshape(4 * ng, 128)
    rows[...] = full_residual

    grad = plane_sum(0, backward())
    residual = field[...]
    moments = direction = pull = jnp.zeros((8, 128), F32)
    image = jnp.zeros((4, 128), F32)
    full_image = jnp.zeros((4 * ng, 128), F32)
    gamma = jnp.ones((1, 1), F32)
    delta = jnp.zeros((1, 1), F32)
    for it in range(ITERS):
        broadcast_lanes(grad)
        push = forward(it)
        if it + 1 < ITERS:
            gather_send[it + 1] = push
            gather(it + 1)
            gather_wait(it + 1)
            full = gathered[it + 1].reshape(4 * ng, 128)
            rows[...] = full
            sums = [full_sum(full_residual * full), full_sum(full * full)]
            if it > 0:
                sums.append(full_sum(full * full_image))
            tile = backward()
            for i, value in enumerate(sums):
                tile = jnp.where(lane == 96 + i, value, tile)
            tile = plane_sum(it + 1, tile)
            gamma_new, delta_new = tile[0:1, 96:97], tile[0:1, 97:98]
            tile_grad = jnp.where(lane >= 96, 0.0, tile)
            if it == 0:
                direction, pull, image, full_image, delta = grad, tile_grad, push, full, delta_new
            else:
                beta = gamma_new / gamma
                delta = delta_new + 2.0 * beta * tile[0:1, 98:99] + beta * beta * delta
                direction = grad + beta * direction
                pull = tile_grad + beta * pull
                image = push + beta * image
                full_image = full + beta * full_image
            gamma = gamma_new
            alpha = gamma / delta
            moments = moments + alpha * direction
            residual = residual - alpha * image
            full_residual = full_residual - alpha * full_image
            grad = grad - alpha * pull
        else:
            spot = lax.broadcasted_iota(jnp.int32, (1, 128), 1)
            sums = jnp.zeros((1, 128), F32)
            for i, other in enumerate((residual, push, image)):
                sums = jnp.where(spot == i, full_sum(push * other), sums)
            norm_send[...] = sums
            to_planes(norm_send, lambda i: norm_recv.at[i], last_sem.at[0], last_sem.at[1])
            moments_flat, direction_flat, grad_flat = from_tile(moments), from_tile(direction), from_tile(grad)
            wait(norm_recv, last_sem.at[1])
            sums = sums + jnp.sum(norm_recv[...], axis=0)
            total_send[...] = sums
            to_grains(lambda peer: total_send, lambda i: total_recv.at[i], last_sem.at[2], last_sem.at[3])
            wait(total_recv, last_sem.at[3])
            sums = sums + jnp.sum(total_recv[...], axis=0)
            beta = sums[:, 0:1] / gamma
            delta = sums[:, 1:2] + 2.0 * beta * sums[:, 2:3] + beta * beta * delta
            alpha = sums[:, 0:1] / delta
            moments_out[...] = moments_flat + alpha * (grad_flat + beta * direction_flat)
            residual_out[...] = residual - alpha * (push + beta * image)

    for it in range(ITERS):
        wait(gathered.at[it, pl.ds(0, ng - 1)], gather_sem.at[0, it])
        wait(part_recv.at[it], part_sem.at[0, it])
        wait(grad_recv.at[it], grad_sem.at[0, it])
    wait(norm_recv, last_sem.at[0])
    wait(total_recv, last_sem.at[2])


def local(sizes, field, grain_positions, pixel_coords, block_grain, block_pixel, block_count):
    nx, nz, npl = sizes
    ng = nx * nz
    vmem = pl.BlockSpec(memory_space=pltpu.VMEM)
    moments, residual = pl.pallas_call(
        functools.partial(kernel, sizes),
        out_shape=(jax.ShapeDtypeStruct((3, 256), F32), jax.ShapeDtypeStruct((4, 128), F32)),
        in_specs=[pl.BlockSpec(memory_space=pl.ANY)] * 6,
        out_specs=(vmem, vmem),
        scratch_shapes=[
            pltpu.VMEM((4, 128), F32),
            pltpu.VMEM((3, 256), jnp.int32),
            pltpu.VMEM((3, ng * 512), jnp.int32),
            pltpu.VMEM((1, SLOTS), jnp.int32),
            pltpu.VMEM((1, SLOTS), jnp.int32),
            pltpu.VMEM((1, 1), jnp.int32),
            pltpu.VMEM((8, 128), jnp.int32),
            pltpu.SMEM((8, 128), jnp.int32),
            pltpu.VMEM((3, 4 * ng, 128), F32),
            pltpu.VMEM((SLOTS, 3, GROUPS, 2, 8, 128), F32),
            pltpu.VMEM((4, 3, GROUPS, 8, 128), F32),
            pltpu.VMEM((SLOTS, 24, 8, 128), F32),
            pltpu.VMEM((4 * ng, 128), F32),
            pltpu.VMEM((3, 256, 128), F32),
            pltpu.VMEM((128, 128), F32),
            pltpu.VMEM((4 * ng, 128), F32),
            pltpu.VMEM((ITERS, 4, 128), F32),
            pltpu.VMEM((ITERS, ng, 4, 128), F32),
            pltpu.VMEM((ITERS, ng, 4, 128), F32),
            pltpu.VMEM((ITERS, ng - 1, 4, 128), F32),
            pltpu.VMEM((ITERS, 8, 128), F32),
            pltpu.VMEM((ITERS, npl - 1, 8, 128), F32),
            pltpu.VMEM((1, 128), F32),
            pltpu.VMEM((npl - 1, 1, 128), F32),
            pltpu.VMEM((1, 128), F32),
            pltpu.VMEM((ng - 1, 1, 128), F32),
            pltpu.SemaphoreType.DMA((2, ITERS)),
            pltpu.SemaphoreType.DMA((2, ITERS)),
            pltpu.SemaphoreType.DMA((2, ITERS)),
            pltpu.SemaphoreType.DMA((4,)),
            pltpu.SemaphoreType.DMA((7,)),
        ],
        compiler_params=pltpu.CompilerParams(collective_id=1, has_side_effects=True, vmem_limit_bytes=40 << 20),
        name="solve",
    )(field.reshape(4, 128), grain_positions, pixel_coords, block_grain, block_pixel, block_count)
    return moments, residual.reshape(512)


def solution(mesh, rows=4):
    grain, plane = mesh.shape["grain"], mesh.shape["plane"]
    placed = (
        P(("plane", "grain")),
        P(None, "grain"),
        P(None, "plane"),
        P("plane", "grain"),
        P("plane", "grain"),
        P("plane", "grain"),
    )
    return jax.shard_map(
        functools.partial(local, (rows, grain // rows, plane)),
        mesh=mesh,
        in_specs=placed,
        out_specs=(P(None, "grain"), P(("plane", "grain"))),
        check_vma=False,
    )
```

```python
import functools

import jax
import jax.numpy as jnp
from jax import lax
from jax.experimental import pallas as pl
from jax.experimental.pallas import tpu as pltpu
from jax.sharding import PartitionSpec as P

MESH = pl.DeviceIdType.MESH
BLOCK_G = 64
ITERS = 3
SLOTS = 36
UNROLL = 4
GROUPS = 8
F32 = jnp.float32


def kernel(
    sizes,
    field_in,
    grains_in,
    pixels_in,
    block_grain_in,
    block_pixel_in,
    block_count_in,
    moments_out,
    residual_out,
    field,
    grains,
    pixels,
    block_grain,
    block_pixel,
    block_count,
    table_made,
    table,
    coords,
    sens,
    spread,
    snap,
    picks,
    unfold,
    contrib,
    rows,
    gather_send,
    gathered,
    part_send,
    part_recv,
    grad_send,
    grad_along,
    grad_passed,
    norm_send,
    norm_along,
    norm_passed,
    total_send,
    total_recv,
    gather_sem,
    part_sem,
    grad_sem,
    last_sem,
    total_sem,
    local_sem,
):
    nx, nz, npl = sizes
    ng = nx * nz
    far = nz // 2
    g, p = lax.axis_index("grain"), lax.axis_index("plane")
    x, z = g // nz, lax.rem(g, nz)
    ny = npl // 2
    y, core = p // 2, lax.rem(p, 2)

    columns = [lax.rem(x + a, nx) * nz for a in range(nx)]
    across = sorted(range(nx), key=lambda a: -min(a, nx - a))

    def grain_peers(body):
        def far_row(m, carry):
            d = far + (1 - 2 * lax.rem(m, 2)) * ((m + 1) // 2)
            row = lax.rem(z + d, nz)
            for a in across:
                body(m * nx + a, columns[a] + row)
            return carry

        lax.fori_loop(0, nz - 1, far_row, 0)
        for a in across[:-1]:
            body((nz - 1) * nx + a - 1, columns[a] + z)

    y_peers = [lax.rem(y + i, ny) * 2 + core for i in sorted(range(1, ny), key=lambda i: -min(i, ny - i))]
    partner = p + 1 - 2 * core

    def each(n, body):
        def step(i, carry):
            body(i)
            return carry

        lax.fori_loop(0, n, step, 0)

    def to_grains(source, place, send_sem, recv_sem):
        def send(i, peer):
            pltpu.make_async_remote_copy(
                src_ref=source(peer),
                dst_ref=place(i),
                send_sem=send_sem,
                recv_sem=recv_sem,
                device_id=(peer, p),
                device_id_type=MESH,
            ).start()

        grain_peers(send)

    def plane_sum(value, sent, along, passed, sems):
        sent[...] = value
        for peer in y_peers:
            pltpu.make_async_remote_copy(
                src_ref=sent,
                dst_ref=along.at[y],
                send_sem=sems.at[0],
                recv_sem=sems.at[1],
                device_id=(g, peer),
                device_id_type=MESH,
            ).start()
        along[y] = value
        wait(along.at[pl.ds(0, ny - 1)], sems.at[1])
        value = jnp.sum(along[...], axis=0)
        passed[0] = value
        pltpu.make_async_remote_copy(
            src_ref=passed.at[0],
            dst_ref=passed.at[1],
            send_sem=sems.at[2],
            recv_sem=sems.at[3],
            device_id=(g, partner),
            device_id_type=MESH,
        ).start()
        wait(passed.at[1], sems.at[3])
        return value + passed[1]

    def wait(ref, sem):
        pltpu.make_async_copy(ref, ref, sem).wait()

    barrier = pltpu.get_barrier_semaphore()
    grain_peers(lambda i, peer: pl.semaphore_signal(barrier, inc=1, device_id=(peer, p), device_id_type=MESH))
    for peer in (*y_peers, partner):
        pl.semaphore_signal(barrier, inc=1, device_id=(g, peer), device_id_type=MESH)
    loads = [
        pltpu.make_async_copy(src, dst, local_sem.at[i])
        for i, (src, dst) in enumerate(
            [
                (block_grain_in, block_grain),
                (block_pixel_in, block_pixel),
                (block_count_in, block_count),
                (grains_in, grains),
                (pixels_in, pixels),
                (field_in, field),
            ]
        )
    ]
    for load in loads:
        load.start()
    for load in loads:
        load.wait()

    lane = lax.broadcasted_iota(jnp.int32, (8, 128), 1)

    def broadcast_lanes(tile):
        for r in range(96):
            c, b, k = r // 32, r // 8 % 4, r % 8
            spread[b, c, k] = jnp.broadcast_to(tile[:, r : r + 1], (8, 128))

    sub, col = (lax.broadcasted_iota(jnp.int32, (40, 128), i) for i in range(2))
    slot = jnp.where(col < 64, col, col - 64)
    row = lax.broadcasted_iota(jnp.int32, (1, 128), 1)
    edge = lax.broadcasted_iota(jnp.int32, (1, SLOTS), 1)
    count = block_count[...]

    def wide(value, fill):
        return jnp.concatenate([value, jnp.full((1, 128 - SLOTS), fill, jnp.int32)], axis=1)

    def upright(value):
        return jnp.sum(jnp.where(sub == col, value, 0), axis=1, keepdims=True)

    def over_slots(value):
        return jnp.sum(value, axis=0, keepdims=True)

    key = wide(jnp.where(edge < count, block_grain[...], 4), 5)
    key_up = upright(key)
    real = sub[:, 0:1] < SLOTS
    ahead = (key < key_up) | ((key == key_up) & (col < sub))
    rank = jnp.sum(ahead.astype(jnp.int32), axis=1, keepdims=True)
    place = (rank == slot) & real
    pixel = over_slots(jnp.where(place, upright(wide(block_pixel[...], 0)), 0))
    block = over_slots(jnp.where(place, key_up, 0))
    alive = over_slots(jnp.where(place & (key_up < 4), 1, 0))
    block = jnp.minimum(block, 3)
    below = over_slots(jnp.where((key_up < block) & real, 1, 0))
    same = jnp.where((row > 0) & ((row > below) | (alive == 0)), 1, 0)
    upto = over_slots(jnp.where((key_up <= row) & real, 1, 0))
    held = over_slots(jnp.where((key_up == row) & real, 1, 0))
    zero = jnp.zeros((1, 128), jnp.int32)
    table_made[...] = jnp.concatenate(
        [pixel, block, alive, same, jnp.maximum(upto - 1, 0), jnp.minimum(held, 1), zero, zero], axis=0
    )
    to_scalars = pltpu.make_async_copy(table_made, table, local_sem.at[6])
    to_scalars.start()
    target = jnp.where(alive > 0, 2 * pixel + jnp.where(row < 64, 0, 1), -1)
    picks[...] = (lax.broadcasted_iota(jnp.int32, (4 * ng, 128), 0) == target).astype(F32)

    grain_s = lax.broadcasted_iota(jnp.int32, (8, 256), 0) == lax.rem(lax.broadcasted_iota(jnp.int32, (8, 256), 1), 8)

    def product(a, b, over):
        return lax.dot_general(
            a, b, (((1,), (over,)), ((), ())), precision=lax.Precision.HIGHEST, preferred_element_type=F32
        )

    for c in range(3):
        eighth = lax.broadcasted_iota(jnp.int32, (256, 128), 0) // 8
        unfold[c] = (eighth + 32 * c == lax.broadcasted_iota(jnp.int32, (256, 128), 1)).astype(F32)

    def to_tile(value):
        return sum(product(jnp.where(grain_s, value[c : c + 1, :], 0.0), unfold[c], 0) for c in range(3))

    def from_tile(tile):
        parts = [jnp.sum(jnp.where(grain_s, product(tile, unfold[c], 1), 0.0), axis=0, keepdims=True) for c in range(3)]
        return jnp.concatenate(parts, axis=0)

    broadcast_lanes(to_tile(grains[...].astype(F32) * 0.03125))
    contrib[...] = jnp.zeros((128, 128), F32)

    for c in range(3):
        coords[c] = (pixels[c : c + 1, :].astype(F32) * 0.03125).reshape(4 * ng, 128)

    def make_sens(j):
        e, b = table[0, j], table[1, j]
        scale = table[2, j].astype(F32) * 27.0
        for h in range(2):
            px, py, pz = (coords[c, pl.ds(2 * e + h, 1), :] for c in range(3))
            for k in range(GROUPS):
                dx = px - spread[b, 0, k]
                dy = py - spread[b, 1, k]
                dz = pz - spread[b, 2, k]
                inv = lax.rsqrt(dx * dx + dy * dy + dz * dz)
                inv2 = inv * inv
                inv3 = inv2 * inv * scale
                along = 3.0 * dz * inv2 * inv3
                sens[j, 0, k, h] = along * dx
                sens[j, 1, k, h] = along * dy
                sens[j, 2, k, h] = along * dz - inv3

    def gather(it):
        to_grains(lambda peer: gather_send.at[it], lambda i: gathered.at[it, g], gather_sem.at[0, it], gather_sem.at[1, it])
        gathered[it, g] = gather_send[it]

    def gather_wait(it):
        wait(gathered.at[it, pl.ds(0, ng - 1)], gather_sem.at[1, it])

    def unrolled(step):
        def several(i, carry):
            for u in range(UNROLL):
                carry = step(i * UNROLL + u, carry)
            return carry

        return several

    def backward():
        def step(j, acc):
            e = table[0, j]
            keep = table[3, j].astype(F32)
            v0 = jnp.broadcast_to(rows[pl.ds(2 * e, 1), :], (8, 128))
            v1 = jnp.broadcast_to(rows[pl.ds(2 * e + 1, 1), :], (8, 128))
            out = []
            for c in range(3):
                for k in range(GROUPS):
                    i = c * GROUPS + k
                    t = acc[i] * keep + (sens[j, c, k, 0] * v0 + sens[j, c, k, 1] * v1)
                    snap[j, i] = t
                    out.append(t)
            return tuple(out)

        lax.fori_loop(0, SLOTS // UNROLL, unrolled(step), tuple(jnp.zeros((8, 128), F32) for _ in range(24)))
        total = jnp.zeros((8, 128), F32)
        for b in range(4):
            last = table[4, b]
            held = table[5, b].astype(F32)
            for i in range(24):
                s = jnp.sum(snap[last, i], axis=1, keepdims=True) * held
                total = jnp.where(lane == (i // 8) * 32 + b * 8 + i % 8, s, total)
        return total

    def forward(it):
        def step(j, carry):
            b = table[1, j]
            acc = [[jnp.zeros((8, 128), F32) for _ in range(2)] for _ in range(2)]
            for c in range(3):
                for k in range(GROUPS):
                    d = spread[b, c, k]
                    for h in range(2):
                        acc[h][k % 2] = acc[h][k % 2] + sens[j, c, k, h] * d
            for h in range(2):
                contrib[pl.ds(64 * h + j, 1), :] = jnp.sum(acc[h][0] + acc[h][1], axis=0, keepdims=True)
            return carry

        lax.fori_loop(0, SLOTS // UNROLL, unrolled(step), 0)
        part = jnp.dot(picks[...], contrib[...], precision=lax.Precision.HIGHEST, preferred_element_type=F32)
        part_send[it] = part.reshape(ng, 4, 128)
        to_grains(lambda peer: part_send.at[it, peer], lambda i: part_recv.at[it, i], part_sem.at[0, it], part_sem.at[1, it])
        wait(part_recv.at[it], part_sem.at[1, it])
        return jnp.sum(part_recv[it], axis=0) + part_send[it, g]

    def grad_sum(it, tile):
        return plane_sum(tile, grad_send.at[it], grad_along.at[it], grad_passed.at[it], grad_sem.at[it])

    def column(value):
        return jnp.sum(jnp.sum(value.reshape(-1, 8, 128), axis=0), axis=1, keepdims=True)

    def full_sum(value):
        return jnp.sum(jnp.sum(value, axis=0, keepdims=True), axis=1, keepdims=True)

    to_scalars.wait()
    pl.semaphore_wait(barrier, ng - 1 + ny)
    gather_send[0] = field[...]
    gather(0)
    each(SLOTS, make_sens)
    gather_wait(0)
    full_residual = gathered[0].reshape(4 * ng, 128)
    rows[...] = full_residual

    grad = grad_sum(0, backward())
    residual = field[...]
    moments = direction = pull = jnp.zeros((8, 128), F32)
    image = jnp.zeros((4, 128), F32)
    full_image = jnp.zeros((4 * ng, 128), F32)
    gamma = jnp.ones((1, 1), F32)
    delta = jnp.zeros((1, 1), F32)
    for it in range(ITERS):
        broadcast_lanes(grad)
        push = forward(it)
        if it + 1 < ITERS:
            gather_send[it + 1] = push
            gather(it + 1)
            gather_wait(it + 1)
            full = gathered[it + 1].reshape(4 * ng, 128)
            rows[...] = full
            sums = [column(full_residual * full), column(full * full)]
            if it > 0:
                sums.append(column(full * full_image))
            tile = backward()
            for i, value in enumerate(sums):
                tile = jnp.where(lane == 96 + i, value, tile)
            tile = grad_sum(it + 1, tile)
            totals = jnp.sum(tile, axis=0, keepdims=True)
            gamma_new, delta_new = totals[:, 96:97], totals[:, 97:98]
            tile_grad = jnp.where(lane >= 96, 0.0, tile)
            if it == 0:
                direction, pull, image, full_image, delta = grad, tile_grad, push, full, delta_new
            else:
                beta = gamma_new / gamma
                delta = delta_new + 2.0 * beta * totals[:, 98:99] + beta * beta * delta
                direction = grad + beta * direction
                pull = tile_grad + beta * pull
                image = push + beta * image
                full_image = full + beta * full_image
            gamma = gamma_new
            alpha = gamma / delta
            moments = moments + alpha * direction
            residual = residual - alpha * image
            full_residual = full_residual - alpha * full_image
            grad = grad - alpha * pull
        else:
            spot = lax.broadcasted_iota(jnp.int32, (1, 128), 1)
            sums = jnp.zeros((1, 128), F32)
            for i, other in enumerate((residual, push, image)):
                sums = jnp.where(spot == i, full_sum(push * other), sums)
            moments_flat, direction_flat, grad_flat = from_tile(moments), from_tile(direction), from_tile(grad)
            sums = plane_sum(sums, norm_send, norm_along, norm_passed, last_sem)
            total_send[...] = sums
            total_recv[g] = sums
            to_grains(lambda peer: total_send, lambda i: total_recv.at[g], total_sem.at[0], total_sem.at[1])
            wait(total_recv.at[pl.ds(0, ng - 1)], total_sem.at[1])
            sums = jnp.sum(total_recv[...], axis=0)
            beta = sums[:, 0:1] / gamma
            delta = sums[:, 1:2] + 2.0 * beta * sums[:, 2:3] + beta * beta * delta
            alpha = sums[:, 0:1] / delta
            moments_out[...] = moments_flat + alpha * (grad_flat + beta * direction_flat)
            residual_out[...] = residual - alpha * (push + beta * image)

    for it in range(ITERS):
        wait(gathered.at[it, pl.ds(0, ng - 1)], gather_sem.at[0, it])
        wait(part_recv.at[it], part_sem.at[0, it])
        wait(grad_along.at[it, pl.ds(0, ny - 1)], grad_sem.at[it, 0])
        wait(grad_passed.at[it, 0], grad_sem.at[it, 2])
    wait(norm_along.at[pl.ds(0, ny - 1)], last_sem.at[0])
    wait(norm_passed.at[0], last_sem.at[2])
    wait(total_recv.at[pl.ds(0, ng - 1)], total_sem.at[0])


def local(sizes, field, grain_positions, pixel_coords, block_grain, block_pixel, block_count):
    nx, nz, npl = sizes
    ng = nx * nz
    vmem = pl.BlockSpec(memory_space=pltpu.VMEM)
    moments, residual = pl.pallas_call(
        functools.partial(kernel, sizes),
        out_shape=(jax.ShapeDtypeStruct((3, 256), F32), jax.ShapeDtypeStruct((4, 128), F32)),
        in_specs=[pl.BlockSpec(memory_space=pltpu.HBM)] * 6,
        out_specs=(vmem, vmem),
        scratch_shapes=[
            pltpu.VMEM((4, 128), F32),
            pltpu.VMEM((3, 256), jnp.int32),
            pltpu.VMEM((3, ng * 512), jnp.int32),
            pltpu.VMEM((1, SLOTS), jnp.int32),
            pltpu.VMEM((1, SLOTS), jnp.int32),
            pltpu.VMEM((1, 1), jnp.int32),
            pltpu.VMEM((8, 128), jnp.int32),
            pltpu.SMEM((8, 128), jnp.int32),
            pltpu.VMEM((3, 4 * ng, 128), F32),
            pltpu.VMEM((SLOTS, 3, GROUPS, 2, 8, 128), F32),
            pltpu.VMEM((4, 3, GROUPS, 8, 128), F32),
            pltpu.VMEM((SLOTS, 24, 8, 128), F32),
            pltpu.VMEM((4 * ng, 128), F32),
            pltpu.VMEM((3, 256, 128), F32),
            pltpu.VMEM((128, 128), F32),
            pltpu.VMEM((4 * ng, 128), F32),
            pltpu.VMEM((ITERS, 4, 128), F32),
            pltpu.VMEM((ITERS, ng, 4, 128), F32),
            pltpu.VMEM((ITERS, ng, 4, 128), F32),
            pltpu.VMEM((ITERS, ng - 1, 4, 128), F32),
            pltpu.VMEM((ITERS, 8, 128), F32),
            pltpu.VMEM((ITERS, npl // 2, 8, 128), F32),
            pltpu.VMEM((ITERS, 2, 8, 128), F32),
            pltpu.VMEM((1, 128), F32),
            pltpu.VMEM((npl // 2, 1, 128), F32),
            pltpu.VMEM((2, 1, 128), F32),
            pltpu.VMEM((1, 128), F32),
            pltpu.VMEM((ng, 1, 128), F32),
            pltpu.SemaphoreType.DMA((2, ITERS)),
            pltpu.SemaphoreType.DMA((2, ITERS)),
            pltpu.SemaphoreType.DMA((ITERS, 4)),
            pltpu.SemaphoreType.DMA((4,)),
            pltpu.SemaphoreType.DMA((2,)),
            pltpu.SemaphoreType.DMA((7,)),
        ],
        compiler_params=pltpu.CompilerParams(collective_id=1, has_side_effects=True, vmem_limit_bytes=60 << 20),
        name="solve",
    )(field.reshape(4, 128), grain_positions, pixel_coords, block_grain, block_pixel, block_count)
    return moments, residual.reshape(512)


def solution(mesh, rows=4):
    grain, plane = mesh.shape["grain"], mesh.shape["plane"]
    placed = (
        P(("plane", "grain")),
        P(None, "grain"),
        P(None, "plane"),
        P("plane", "grain"),
        P("plane", "grain"),
        P("plane", "grain"),
    )
    return jax.shard_map(
        functools.partial(local, (rows, grain // rows, plane)),
        mesh=mesh,
        in_specs=placed,
        out_specs=(P(None, "grain"), P(("plane", "grain"))),
        check_vma=False,
    )
```

```python
import functools

import jax
import jax.numpy as jnp
from jax import lax
from jax.experimental import pallas as pl
from jax.experimental.pallas import tpu as pltpu
from jax.sharding import PartitionSpec as P

MESH = pl.DeviceIdType.MESH
BLOCK_G = 64
ITERS = 3
SLOTS = 36
UNROLL = 6
GROUPS = 8
F32 = jnp.float32


def kernel(
    sizes,
    field_in,
    grains_in,
    pixels_in,
    block_grain_in,
    block_pixel_in,
    block_count_in,
    moments_out,
    residual_out,
    field,
    grains,
    pixels,
    block_grain,
    block_pixel,
    block_count,
    table_made,
    table,
    coords,
    sens,
    spread,
    snap,
    picks,
    unfold,
    contrib,
    rows,
    full_residual,
    full_image,
    gather_send,
    gathered,
    part_send,
    part_recv,
    grad_send,
    grad_recv,
    norm_send,
    norm_recv,
    total_send,
    total_recv,
    gather_sem,
    part_sem,
    grad_sem,
    last_sem,
    total_sem,
    local_sem,
):
    nx, nz, npl = sizes
    ng = nx * nz
    far = nz // 2
    g, p = lax.axis_index("grain"), lax.axis_index("plane")
    x, z = g // nz, lax.rem(g, nz)

    columns = [lax.rem(x + a, nx) * nz for a in range(nx)]
    across = sorted(range(nx), key=lambda a: -min(a, nx - a))

    def grain_peers(body):
        def far_row(m, carry):
            d = far + (1 - 2 * lax.rem(m, 2)) * ((m + 1) // 2)
            row = lax.rem(z + d, nz)
            for a in across:
                body(m * nx + a, columns[a] + row)
            return carry

        lax.fori_loop(0, nz - 1, far_row, 0)
        for a in across[:-1]:
            body((nz - 1) * nx + a - 1, columns[a] + z)

    def plane_peers(body):
        for i in range(1, npl):
            body(lax.rem(p + i, npl))

    def each(n, body):
        def step(i, carry):
            body(i)
            return carry

        lax.fori_loop(0, n, step, 0)

    def to_grains(source, place, send_sem, recv_sem):
        def send(i, peer):
            pltpu.make_async_remote_copy(
                src_ref=source(peer),
                dst_ref=place(i),
                send_sem=send_sem,
                recv_sem=recv_sem,
                device_id=(peer, p),
                device_id_type=MESH,
            ).start()

        grain_peers(send)

    def plane_sum(value, sent, landed, sems):
        sent[...] = value

        def send(peer):
            pltpu.make_async_remote_copy(
                src_ref=sent,
                dst_ref=landed.at[p],
                send_sem=sems.at[0],
                recv_sem=sems.at[1],
                device_id=(g, peer),
                device_id_type=MESH,
            ).start()

        plane_peers(send)
        landed[p] = value
        wait(landed.at[pl.ds(0, npl - 1)], sems.at[1])
        return jnp.sum(landed[...], axis=0)

    def wait(ref, sem):
        pltpu.make_async_copy(ref, ref, sem).wait()

    barrier = pltpu.get_barrier_semaphore()
    grain_peers(lambda i, peer: pl.semaphore_signal(barrier, inc=1, device_id=(peer, p), device_id_type=MESH))
    plane_peers(lambda peer: pl.semaphore_signal(barrier, inc=1, device_id=(g, peer), device_id_type=MESH))
    loads = [
        pltpu.make_async_copy(src, dst, local_sem.at[i])
        for i, (src, dst) in enumerate(
            [
                (block_grain_in, block_grain),
                (block_pixel_in, block_pixel),
                (block_count_in, block_count),
                (grains_in, grains),
                (pixels_in, pixels),
                (field_in, field),
            ]
        )
    ]
    for load in loads:
        load.start()
    for load in loads:
        load.wait()

    lane = lax.broadcasted_iota(jnp.int32, (8, 128), 1)

    def broadcast_lanes(tile):
        for r in range(96):
            c, b, k = r // 32, r // 8 % 4, r % 8
            spread[b, c, k] = jnp.broadcast_to(tile[:, r : r + 1], (8, 128))

    sub, col = (lax.broadcasted_iota(jnp.int32, (40, 128), i) for i in range(2))
    slot = jnp.where(col < 64, col, col - 64)
    row = lax.broadcasted_iota(jnp.int32, (1, 128), 1)
    edge = lax.broadcasted_iota(jnp.int32, (1, SLOTS), 1)
    count = block_count[...]

    def wide(value, fill):
        return jnp.concatenate([value, jnp.full((1, 128 - SLOTS), fill, jnp.int32)], axis=1)

    def upright(value):
        return jnp.sum(jnp.where(sub == col, value, 0), axis=1, keepdims=True)

    def over_slots(value):
        return jnp.sum(value, axis=0, keepdims=True)

    key = wide(jnp.where(edge < count, block_grain[...], 4), 5)
    key_up = upright(key)
    real = sub[:, 0:1] < SLOTS
    ahead = (key < key_up) | ((key == key_up) & (col < sub))
    rank = jnp.sum(ahead.astype(jnp.int32), axis=1, keepdims=True)
    place = (rank == slot) & real
    pixel = over_slots(jnp.where(place, upright(wide(block_pixel[...], 0)), 0))
    block = over_slots(jnp.where(place, key_up, 0))
    alive = over_slots(jnp.where(place & (key_up < 4), 1, 0))
    block = jnp.minimum(block, 3)
    below = over_slots(jnp.where((key_up < block) & real, 1, 0))
    same = jnp.where((row > 0) & ((row > below) | (alive == 0)), 1, 0)
    upto = over_slots(jnp.where((key_up <= row) & real, 1, 0))
    held = over_slots(jnp.where((key_up == row) & real, 1, 0))
    zero = jnp.zeros((1, 128), jnp.int32)
    table_made[...] = jnp.concatenate(
        [pixel, block, alive, same, jnp.maximum(upto - 1, 0), jnp.minimum(held, 1), zero, zero], axis=0
    )
    to_scalars = pltpu.make_async_copy(table_made, table, local_sem.at[6])
    to_scalars.start()
    target = jnp.where(alive > 0, 2 * pixel + jnp.where(row < 64, 0, 1), -1)
    chosen = (lax.broadcasted_iota(jnp.int32, (4 * ng, 128), 0) == target).astype(F32).astype(jnp.bfloat16)
    for i in range(3):
        picks[:, 128 * i : 128 * (i + 1)] = chosen

    grain_s = lax.broadcasted_iota(jnp.int32, (8, 256), 0) == lax.rem(lax.broadcasted_iota(jnp.int32, (8, 256), 1), 8)

    def product(a, b, over):
        return lax.dot_general(
            a, b, (((1,), (over,)), ((), ())), precision=lax.Precision.HIGHEST, preferred_element_type=F32
        )

    for c in range(3):
        eighth = lax.broadcasted_iota(jnp.int32, (256, 128), 0) // 8
        unfold[c] = (eighth + 32 * c == lax.broadcasted_iota(jnp.int32, (256, 128), 1)).astype(F32)

    def to_tile(value):
        return sum(product(jnp.where(grain_s, value[c : c + 1, :], 0.0), unfold[c], 0) for c in range(3))

    def from_tile(tile):
        parts = [jnp.sum(jnp.where(grain_s, product(tile, unfold[c], 1), 0.0), axis=0, keepdims=True) for c in range(3)]
        return jnp.concatenate(parts, axis=0)

    broadcast_lanes(to_tile(grains[...].astype(F32) * 0.03125))
    contrib[...] = jnp.zeros((128, 128), F32)

    for c in range(3):
        coords[c] = (pixels[c : c + 1, :].astype(F32) * 0.03125).reshape(4 * ng, 128)

    def make_sens(j):
        e, b = table[0, j], table[1, j]
        scale = table[2, j].astype(F32) * 27.0
        for h in range(2):
            px, py, pz = (coords[c, pl.ds(2 * e + h, 1), :] for c in range(3))
            for k in range(GROUPS):
                dx = px - spread[b, 0, k]
                dy = py - spread[b, 1, k]
                dz = pz - spread[b, 2, k]
                inv = lax.rsqrt(dx * dx + dy * dy + dz * dz)
                inv2 = inv * inv
                inv3 = inv2 * inv * scale
                along = 3.0 * dz * inv2 * inv3
                sens[j, 0, k, h] = along * dx
                sens[j, 1, k, h] = along * dy
                sens[j, 2, k, h] = along * dz - inv3

    def gather(it):
        to_grains(lambda peer: gather_send.at[it], lambda i: gathered.at[it, g], gather_sem.at[0, it], gather_sem.at[1, it])
        gathered[it, g] = gather_send[it]

    def gather_wait(it):
        wait(gathered.at[it, pl.ds(0, ng - 1)], gather_sem.at[1, it])

    def unrolled(step):
        def several(i, carry):
            for u in range(UNROLL):
                carry = step(i * UNROLL + u, carry)
            return carry

        return several

    def backward():
        def step(j, acc):
            e = table[0, j]
            keep = table[3, j].astype(F32)
            v0 = jnp.broadcast_to(rows[pl.ds(2 * e, 1), :], (8, 128))
            v1 = jnp.broadcast_to(rows[pl.ds(2 * e + 1, 1), :], (8, 128))
            out = []
            for c in range(3):
                for k in range(GROUPS):
                    i = c * GROUPS + k
                    t = acc[i] * keep + (sens[j, c, k, 0] * v0 + sens[j, c, k, 1] * v1)
                    snap[j, i] = t
                    out.append(t)
            return tuple(out)

        lax.fori_loop(0, SLOTS // UNROLL, unrolled(step), tuple(jnp.zeros((8, 128), F32) for _ in range(24)))
        total = jnp.zeros((8, 128), F32)
        for b in range(4):
            last = table[4, b]
            held = table[5, b].astype(F32)
            for i in range(24):
                s = jnp.sum(snap[last, i], axis=1, keepdims=True) * held
                total = jnp.where(lane == (i // 8) * 32 + b * 8 + i % 8, s, total)
        return total

    def forward(it, meanwhile):
        def step(j, carry):
            b = table[1, j]
            acc = [[jnp.zeros((8, 128), F32) for _ in range(2)] for _ in range(2)]
            for c in range(3):
                for k in range(GROUPS):
                    d = spread[b, c, k]
                    for h in range(2):
                        acc[h][k % 2] = acc[h][k % 2] + sens[j, c, k, h] * d
            for h in range(2):
                contrib[pl.ds(64 * h + j, 1), :] = jnp.sum(acc[h][0] + acc[h][1], axis=0, keepdims=True)
            return carry

        lax.fori_loop(0, SLOTS // UNROLL, unrolled(step), 0)
        value = contrib[...]
        high = value.astype(jnp.bfloat16)
        rest = value - high.astype(F32)
        middle = rest.astype(jnp.bfloat16)
        low = (rest - middle.astype(F32)).astype(jnp.bfloat16)
        pieces = jnp.concatenate([high, middle, low], axis=0)
        part = jnp.dot(picks[...], pieces, preferred_element_type=F32)
        part_send[it] = part.reshape(ng, 4, 128)
        to_grains(lambda peer: part_send.at[it, peer], lambda i: part_recv.at[it, i], part_sem.at[0, it], part_sem.at[1, it])
        meanwhile()
        wait(part_recv.at[it], part_sem.at[1, it])
        return jnp.sum(part_recv[it], axis=0) + part_send[it, g]

    def grad_sum(it, tile):
        return plane_sum(tile, grad_send.at[it], grad_recv.at[it], grad_sem.at[it])

    def column(value):
        return jnp.sum(jnp.sum(value.reshape(-1, 8, 128), axis=0), axis=1, keepdims=True)

    def full_sum(value):
        return jnp.sum(jnp.sum(value, axis=0, keepdims=True), axis=1, keepdims=True)

    to_scalars.wait()
    pl.semaphore_wait(barrier, ng - 1 + npl - 1)
    gather_send[0] = field[...]
    gather(0)
    each(SLOTS, make_sens)
    gather_wait(0)
    rows[...] = gathered[0].reshape(4 * ng, 128)
    full_residual[...] = rows[...]

    grad = grad_sum(0, backward())
    residual = field[...]
    moments = direction = pull = jnp.zeros((8, 128), F32)
    image = jnp.zeros((4, 128), F32)
    gamma = jnp.ones((1, 1), F32)
    alpha = beta = delta = jnp.zeros((1, 1), F32)
    full_image[...] = jnp.zeros((4 * ng, 128), F32)
    for it in range(ITERS):
        broadcast_lanes(grad)

        def meanwhile():
            if 0 < it < ITERS - 1:
                full_image[...] = rows[...] + beta * full_image[...]
                full_residual[...] = full_residual[...] - alpha * full_image[...]

        push = forward(it, meanwhile)
        if it + 1 < ITERS:
            gather_send[it + 1] = push
            gather(it + 1)
            gather_wait(it + 1)
            full = gathered[it + 1].reshape(4 * ng, 128)
            rows[...] = full
            sums = [column(full_residual[...] * full), column(full * full), column(full * full_image[...])]
            tile = backward()
            for i, value in enumerate(sums):
                tile = jnp.where(lane == 96 + i, value, tile)
            tile = grad_sum(it + 1, tile)
            totals = jnp.sum(tile, axis=0, keepdims=True)
            gamma_new = totals[:, 96:97]
            beta = gamma_new / gamma if it > 0 else jnp.zeros((1, 1), F32)
            delta = totals[:, 97:98] + 2.0 * beta * totals[:, 98:99] + beta * beta * delta
            gamma = gamma_new
            alpha = gamma / delta
            pull = jnp.where(lane >= 96, 0.0, tile) + beta * pull
            direction = grad + beta * direction
            moments = moments + alpha * direction
            image = push + beta * image
            residual = residual - alpha * image
            grad = grad - alpha * pull
        else:
            spot = lax.broadcasted_iota(jnp.int32, (1, 128), 1)
            sums = jnp.zeros((1, 128), F32)
            for i, other in enumerate((residual, push, image)):
                sums = jnp.where(spot == i, full_sum(push * other), sums)
            sums = plane_sum(sums, norm_send, norm_recv, last_sem)
            total_send[...] = sums
            total_recv[g] = sums
            to_grains(lambda peer: total_send, lambda i: total_recv.at[g], total_sem.at[0], total_sem.at[1])
            moments_flat, direction_flat, grad_flat = from_tile(moments), from_tile(direction), from_tile(grad)
            wait(total_recv.at[pl.ds(0, ng - 1)], total_sem.at[1])
            sums = jnp.sum(total_recv[...], axis=0)
            beta = sums[:, 0:1] / gamma
            delta = sums[:, 1:2] + 2.0 * beta * sums[:, 2:3] + beta * beta * delta
            alpha = sums[:, 0:1] / delta
            moments_out[...] = moments_flat + alpha * (grad_flat + beta * direction_flat)
            residual_out[...] = residual - alpha * (push + beta * image)

    for it in range(ITERS):
        wait(gathered.at[it, pl.ds(0, ng - 1)], gather_sem.at[0, it])
        wait(part_recv.at[it], part_sem.at[0, it])
        wait(grad_recv.at[it, pl.ds(0, npl - 1)], grad_sem.at[it, 0])
    wait(norm_recv.at[pl.ds(0, npl - 1)], last_sem.at[0])
    wait(total_recv.at[pl.ds(0, ng - 1)], total_sem.at[0])


def local(sizes, field, grain_positions, pixel_coords, block_grain, block_pixel, block_count):
    nx, nz, npl = sizes
    ng = nx * nz
    vmem = pl.BlockSpec(memory_space=pltpu.VMEM)
    moments, residual = pl.pallas_call(
        functools.partial(kernel, sizes),
        out_shape=(jax.ShapeDtypeStruct((3, 256), F32), jax.ShapeDtypeStruct((4, 128), F32)),
        in_specs=[pl.BlockSpec(memory_space=pltpu.HBM)] * 6,
        out_specs=(vmem, vmem),
        scratch_shapes=[
            pltpu.VMEM((4, 128), F32),
            pltpu.VMEM((3, 256), jnp.int32),
            pltpu.VMEM((3, ng * 512), jnp.int32),
            pltpu.VMEM((1, SLOTS), jnp.int32),
            pltpu.VMEM((1, SLOTS), jnp.int32),
            pltpu.VMEM((1, 1), jnp.int32),
            pltpu.VMEM((8, 128), jnp.int32),
            pltpu.SMEM((8, 128), jnp.int32),
            pltpu.VMEM((3, 4 * ng, 128), F32),
            pltpu.VMEM((SLOTS, 3, GROUPS, 2, 8, 128), F32),
            pltpu.VMEM((4, 3, GROUPS, 8, 128), F32),
            pltpu.VMEM((SLOTS, 24, 8, 128), F32),
            pltpu.VMEM((4 * ng, 384), jnp.bfloat16),
            pltpu.VMEM((3, 256, 128), F32),
            pltpu.VMEM((128, 128), F32),
            pltpu.VMEM((4 * ng, 128), F32),
            pltpu.VMEM((4 * ng, 128), F32),
            pltpu.VMEM((4 * ng, 128), F32),
            pltpu.VMEM((ITERS, 4, 128), F32),
            pltpu.VMEM((ITERS, ng, 4, 128), F32),
            pltpu.VMEM((ITERS, ng, 4, 128), F32),
            pltpu.VMEM((ITERS, ng - 1, 4, 128), F32),
            pltpu.VMEM((ITERS, 8, 128), F32),
            pltpu.VMEM((ITERS, npl, 8, 128), F32),
            pltpu.VMEM((1, 128), F32),
            pltpu.VMEM((npl, 1, 128), F32),
            pltpu.VMEM((1, 128), F32),
            pltpu.VMEM((ng, 1, 128), F32),
            pltpu.SemaphoreType.DMA((2, ITERS)),
            pltpu.SemaphoreType.DMA((2, ITERS)),
            pltpu.SemaphoreType.DMA((ITERS, 2)),
            pltpu.SemaphoreType.DMA((2,)),
            pltpu.SemaphoreType.DMA((2,)),
            pltpu.SemaphoreType.DMA((7,)),
        ],
        compiler_params=pltpu.CompilerParams(collective_id=1, has_side_effects=True, vmem_limit_bytes=60 << 20),
        name="solve",
    )(field.reshape(4, 128), grain_positions, pixel_coords, block_grain, block_pixel, block_count)
    return moments, residual.reshape(512)


def solution(mesh, rows=4):
    grain, plane = mesh.shape["grain"], mesh.shape["plane"]
    placed = (
        P(("plane", "grain")),
        P(None, "grain"),
        P(None, "plane"),
        P("plane", "grain"),
        P("plane", "grain"),
        P("plane", "grain"),
    )
    return jax.shard_map(
        functools.partial(local, (rows, grain // rows, plane)),
        mesh=mesh,
        in_specs=placed,
        out_specs=(P(None, "grain"), P(("plane", "grain"))),
        check_vma=False,
    )
```

```python
import functools

import jax
import jax.numpy as jnp
from jax import lax
from jax.experimental import pallas as pl
from jax.experimental.pallas import tpu as pltpu
from jax.sharding import PartitionSpec as P

MESH = pl.DeviceIdType.MESH
BLOCK_G = 64
ITERS = 3
SLOTS = 36
UNROLL = 6
GROUPS = 8
F32 = jnp.float32


def kernel(
    sizes,
    field_in,
    grains_in,
    pixels_in,
    block_grain_in,
    block_pixel_in,
    block_count_in,
    moments_out,
    residual_out,
    field,
    grains,
    pixels,
    block_grain,
    block_pixel,
    block_count,
    table_made,
    table,
    coords,
    sens,
    spread,
    snap,
    picks,
    unfold,
    contrib,
    rows,
    full_residual,
    full_image,
    gather_send,
    gathered,
    part_send,
    part_recv,
    grad_send,
    grad_recv,
    norm_send,
    norm_recv,
    total_send,
    total_recv,
    gather_sem,
    part_sem,
    grad_sem,
    last_sem,
    total_sem,
    local_sem,
):
    nx, nz, npl = sizes
    ng = nx * nz
    far = nz // 2
    g, p = lax.axis_index("grain"), lax.axis_index("plane")
    x, z = g // nz, lax.rem(g, nz)

    columns = [lax.rem(x + a, nx) * nz for a in range(nx)]
    across = sorted(range(nx), key=lambda a: -min(a, nx - a))

    def grain_peers(body):
        def far_row(m, carry):
            d = far + (1 - 2 * lax.rem(m, 2)) * ((m + 1) // 2)
            row = lax.rem(z + d, nz)
            for a in across:
                body(m * nx + a, columns[a] + row)
            return carry

        lax.fori_loop(0, nz - 1, far_row, 0)
        for a in across[:-1]:
            body((nz - 1) * nx + a - 1, columns[a] + z)

    def plane_peers(body):
        for i in range(1, npl):
            body(lax.rem(p + i, npl))

    def each(n, body):
        def step(i, carry):
            body(i)
            return carry

        lax.fori_loop(0, n, step, 0)

    def to_grains(source, place, send_sem, recv_sem):
        def send(i, peer):
            pltpu.make_async_remote_copy(
                src_ref=source(peer),
                dst_ref=place(i),
                send_sem=send_sem,
                recv_sem=recv_sem,
                device_id=(peer, p),
                device_id_type=MESH,
            ).start()

        grain_peers(send)

    def plane_sum(value, sent, landed, sems):
        sent[...] = value

        def send(peer):
            pltpu.make_async_remote_copy(
                src_ref=sent,
                dst_ref=landed.at[p],
                send_sem=sems.at[0],
                recv_sem=sems.at[1],
                device_id=(g, peer),
                device_id_type=MESH,
            ).start()

        plane_peers(send)
        landed[p] = value
        wait(landed.at[pl.ds(0, npl - 1)], sems.at[1])
        return jnp.sum(landed[...], axis=0)

    def wait(ref, sem):
        pltpu.make_async_copy(ref, ref, sem).wait()

    barrier = pltpu.get_barrier_semaphore()
    grain_peers(lambda i, peer: pl.semaphore_signal(barrier, inc=1, device_id=(peer, p), device_id_type=MESH))
    plane_peers(lambda peer: pl.semaphore_signal(barrier, inc=1, device_id=(g, peer), device_id_type=MESH))
    loads = [
        pltpu.make_async_copy(src, dst, local_sem.at[i])
        for i, (src, dst) in enumerate(
            [
                (block_grain_in, block_grain),
                (block_pixel_in, block_pixel),
                (block_count_in, block_count),
                (grains_in, grains),
                (pixels_in, pixels),
                (field_in, field),
            ]
        )
    ]
    for load in loads:
        load.start()
    for load in loads:
        load.wait()

    lane = lax.broadcasted_iota(jnp.int32, (8, 128), 1)

    def broadcast_lanes(tile):
        for r in range(96):
            c, b, k = r // 32, r // 8 % 4, r % 8
            spread[b, c, k] = jnp.broadcast_to(tile[:, r : r + 1], (8, 128))

    sub, col = (lax.broadcasted_iota(jnp.int32, (40, 128), i) for i in range(2))
    slot = jnp.where(col < 64, col, col - 64)
    row = lax.broadcasted_iota(jnp.int32, (1, 128), 1)
    edge = lax.broadcasted_iota(jnp.int32, (1, SLOTS), 1)
    count = block_count[...]

    def wide(value, fill):
        return jnp.concatenate([value, jnp.full((1, 128 - SLOTS), fill, jnp.int32)], axis=1)

    def upright(value):
        return jnp.sum(jnp.where(sub == col, value, 0), axis=1, keepdims=True)

    def over_slots(value):
        return jnp.sum(value, axis=0, keepdims=True)

    key = wide(jnp.where(edge < count, block_grain[...], 4), 5)
    key_up = upright(key)
    real = sub[:, 0:1] < SLOTS
    ahead = (key < key_up) | ((key == key_up) & (col < sub))
    rank = jnp.sum(ahead.astype(jnp.int32), axis=1, keepdims=True)
    place = (rank == slot) & real
    pixel = over_slots(jnp.where(place, upright(wide(block_pixel[...], 0)), 0))
    block = over_slots(jnp.where(place, key_up, 0))
    alive = over_slots(jnp.where(place & (key_up < 4), 1, 0))
    block = jnp.minimum(block, 3)
    below = over_slots(jnp.where((key_up < block) & real, 1, 0))
    same = jnp.where((row > 0) & ((row > below) | (alive == 0)), 1, 0)
    upto = over_slots(jnp.where((key_up <= row) & real, 1, 0))
    held = over_slots(jnp.where((key_up == row) & real, 1, 0))
    zero = jnp.zeros((1, 128), jnp.int32)
    table_made[...] = jnp.concatenate(
        [pixel, block, alive, same, jnp.maximum(upto - 1, 0), jnp.minimum(held, 1), zero, zero], axis=0
    )
    to_scalars = pltpu.make_async_copy(table_made, table, local_sem.at[6])
    to_scalars.start()
    target = jnp.where(alive > 0, 2 * pixel + jnp.where(row < 64, 0, 1), -1)
    chosen = (lax.broadcasted_iota(jnp.int32, (4 * ng, 128), 0) == target).astype(F32).astype(jnp.bfloat16)
    for i in range(3):
        picks[:, 128 * i : 128 * (i + 1)] = chosen

    grain_s = lax.broadcasted_iota(jnp.int32, (8, 256), 0) == lax.rem(lax.broadcasted_iota(jnp.int32, (8, 256), 1), 8)

    def product(a, b, over):
        return lax.dot_general(
            a, b, (((1,), (over,)), ((), ())), precision=lax.Precision.HIGHEST, preferred_element_type=F32
        )

    for c in range(3):
        eighth = lax.broadcasted_iota(jnp.int32, (256, 128), 0) // 8
        unfold[c] = (eighth + 32 * c == lax.broadcasted_iota(jnp.int32, (256, 128), 1)).astype(F32)

    def to_tile(value):
        return sum(product(jnp.where(grain_s, value[c : c + 1, :], 0.0), unfold[c], 0) for c in range(3))

    def from_tile(tile):
        parts = [jnp.sum(jnp.where(grain_s, product(tile, unfold[c], 1), 0.0), axis=0, keepdims=True) for c in range(3)]
        return jnp.concatenate(parts, axis=0)

    broadcast_lanes(to_tile(grains[...].astype(F32) * 0.03125))
    contrib[...] = jnp.zeros((128, 128), F32)

    for c in range(3):
        coords[c] = (pixels[c : c + 1, :].astype(F32) * 0.03125).reshape(4 * ng, 128)

    def make_sens(j):
        e, b = table[0, j], table[1, j]
        scale = table[2, j].astype(F32) * 27.0
        for h in range(2):
            px, py, pz = (coords[c, pl.ds(2 * e + h, 1), :] for c in range(3))
            for k in range(GROUPS):
                dx = px - spread[b, 0, k]
                dy = py - spread[b, 1, k]
                dz = pz - spread[b, 2, k]
                inv = lax.rsqrt(dx * dx + dy * dy + dz * dz)
                inv2 = inv * inv
                inv3 = inv2 * inv * scale
                along = 3.0 * dz * inv2 * inv3
                sens[j, 0, k, h] = along * dx
                sens[j, 1, k, h] = along * dy
                sens[j, 2, k, h] = along * dz - inv3

    def gather(it):
        to_grains(lambda peer: gather_send.at[it], lambda i: gathered.at[it, g], gather_sem.at[0, it], gather_sem.at[1, it])
        gathered[it, g] = gather_send[it]

    def gather_wait(it):
        wait(gathered.at[it, pl.ds(0, ng - 1)], gather_sem.at[1, it])

    def pairwise(values):
        while len(values) > 1:
            values = [sum(values[i : i + 2]) for i in range(0, len(values), 2)]
        return values[0]

    def unrolled(step):
        def several(i, carry):
            for u in range(UNROLL):
                carry = step(i * UNROLL + u, carry)
            return carry

        return several

    def backward():
        def step(j, acc):
            e = table[0, j]
            keep = table[3, j].astype(F32)
            v0 = jnp.broadcast_to(rows[pl.ds(2 * e, 1), :], (8, 128))
            v1 = jnp.broadcast_to(rows[pl.ds(2 * e + 1, 1), :], (8, 128))
            out = []
            for c in range(3):
                for k in range(GROUPS):
                    i = c * GROUPS + k
                    t = acc[i] * keep + (sens[j, c, k, 0] * v0 + sens[j, c, k, 1] * v1)
                    snap[j, i] = t
                    out.append(t)
            return tuple(out)

        lax.fori_loop(0, SLOTS // UNROLL, unrolled(step), tuple(jnp.zeros((8, 128), F32) for _ in range(24)))
        totals = []
        for b in range(4):
            last = table[4, b]
            held = table[5, b].astype(F32)
            for c in range(3):
                part = jnp.zeros((8, 128), F32)
                for k in range(GROUPS):
                    s = jnp.sum(snap[last, c * GROUPS + k], axis=1, keepdims=True)
                    part = jnp.where(lane == c * 32 + b * 8 + k, s, part)
                totals.append(part * held)
        return pairwise(totals)

    def forward(it, meanwhile):
        def step(j, carry):
            b = table[1, j]
            acc = [[jnp.zeros((8, 128), F32) for _ in range(2)] for _ in range(2)]
            for c in range(3):
                for k in range(GROUPS):
                    d = spread[b, c, k]
                    for h in range(2):
                        acc[h][k % 2] = acc[h][k % 2] + sens[j, c, k, h] * d
            for h in range(2):
                contrib[pl.ds(64 * h + j, 1), :] = jnp.sum(acc[h][0] + acc[h][1], axis=0, keepdims=True)
            return carry

        lax.fori_loop(0, SLOTS // UNROLL, unrolled(step), 0)
        value = contrib[...]
        high = value.astype(jnp.bfloat16)
        rest = value - high.astype(F32)
        middle = rest.astype(jnp.bfloat16)
        low = (rest - middle.astype(F32)).astype(jnp.bfloat16)
        pieces = jnp.concatenate([high, middle, low], axis=0)
        part = jnp.dot(picks[...], pieces, preferred_element_type=F32)
        part_send[it] = part.reshape(ng, 4, 128)
        to_grains(lambda peer: part_send.at[it, peer], lambda i: part_recv.at[it, i], part_sem.at[0, it], part_sem.at[1, it])
        meanwhile()
        wait(part_recv.at[it], part_sem.at[1, it])
        chains = [jnp.sum(part_recv[it, i : min(i + 8, ng - 1)], axis=0) for i in range(0, ng - 1, 8)]
        return pairwise(chains) + part_send[it, g]

    def grad_sum(it, tile):
        return plane_sum(tile, grad_send.at[it], grad_recv.at[it], grad_sem.at[it])

    def column(value):
        return jnp.sum(jnp.sum(value.reshape(-1, 8, 128), axis=0), axis=1, keepdims=True)

    def full_sum(value):
        return jnp.sum(jnp.sum(value, axis=0, keepdims=True), axis=1, keepdims=True)

    to_scalars.wait()
    gather_send[0] = field[...]
    pl.semaphore_wait(barrier, ng - 1 + npl - 1)
    gather(0)
    each(SLOTS, make_sens)
    gather_wait(0)
    rows[...] = gathered[0].reshape(4 * ng, 128)
    full_residual[...] = rows[...]

    grad = grad_sum(0, backward())
    residual = field[...]
    moments = direction = pull = jnp.zeros((8, 128), F32)
    image = jnp.zeros((4, 128), F32)
    gamma = jnp.ones((1, 1), F32)
    alpha = beta = delta = jnp.zeros((1, 1), F32)
    full_image[...] = jnp.zeros((4 * ng, 128), F32)
    for it in range(ITERS):
        broadcast_lanes(grad)

        def meanwhile():
            if 0 < it < ITERS - 1:
                full_image[...] = rows[...] + beta * full_image[...]
                full_residual[...] = full_residual[...] - alpha * full_image[...]

        push = forward(it, meanwhile)
        if it + 1 < ITERS:
            gather_send[it + 1] = push
            gather(it + 1)
            gather_wait(it + 1)
            full = gathered[it + 1].reshape(4 * ng, 128)
            rows[...] = full
            sums = [column(full_residual[...] * full), column(full * full), column(full * full_image[...])]
            tile = backward()
            for i, value in enumerate(sums):
                tile = jnp.where(lane == 96 + i, value, tile)
            tile = grad_sum(it + 1, tile)
            totals = jnp.sum(tile, axis=0, keepdims=True)
            gamma_new = totals[:, 96:97]
            beta = gamma_new / gamma if it > 0 else jnp.zeros((1, 1), F32)
            delta = totals[:, 97:98] + 2.0 * beta * totals[:, 98:99] + beta * beta * delta
            gamma = gamma_new
            alpha = gamma / delta
            pull = jnp.where(lane >= 96, 0.0, tile) + beta * pull
            direction = grad + beta * direction
            moments = moments + alpha * direction
            image = push + beta * image
            residual = residual - alpha * image
            grad = grad - alpha * pull
        else:
            spot = lax.broadcasted_iota(jnp.int32, (1, 128), 1)
            sums = jnp.zeros((1, 128), F32)
            for i, other in enumerate((residual, push, image)):
                sums = jnp.where(spot == i, full_sum(push * other), sums)
            sums = plane_sum(sums, norm_send, norm_recv, last_sem)
            total_send[...] = sums
            total_recv[g] = sums
            to_grains(lambda peer: total_send, lambda i: total_recv.at[g], total_sem.at[0], total_sem.at[1])
            moments_flat, direction_flat, grad_flat = from_tile(moments), from_tile(direction), from_tile(grad)
            wait(total_recv.at[pl.ds(0, ng - 1)], total_sem.at[1])
            sums = pairwise([jnp.sum(total_recv[i : i + 8], axis=0) for i in range(0, ng, 8)])
            beta = sums[:, 0:1] / gamma
            delta = sums[:, 1:2] + 2.0 * beta * sums[:, 2:3] + beta * beta * delta
            alpha = sums[:, 0:1] / delta
            moments_out[...] = moments_flat + alpha * (grad_flat + beta * direction_flat)
            residual_out[...] = residual - alpha * (push + beta * image)

    for it in range(ITERS):
        wait(gathered.at[it, pl.ds(0, ng - 1)], gather_sem.at[0, it])
        wait(part_recv.at[it], part_sem.at[0, it])
        wait(grad_recv.at[it, pl.ds(0, npl - 1)], grad_sem.at[it, 0])
    wait(norm_recv.at[pl.ds(0, npl - 1)], last_sem.at[0])
    wait(total_recv.at[pl.ds(0, ng - 1)], total_sem.at[0])


def hand_on(moments, residual, moments_out, residual_out, sems):
    copies = [
        pltpu.make_async_copy(moments, moments_out, sems.at[0]),
        pltpu.make_async_copy(residual, residual_out, sems.at[1]),
    ]
    for copy in copies:
        copy.start()
    for copy in copies:
        copy.wait()


def local(sizes, field, grain_positions, pixel_coords, block_grain, block_pixel, block_count):
    nx, nz, npl = sizes
    ng = nx * nz
    vmem = pl.BlockSpec(memory_space=pltpu.VMEM)
    moments, residual = pl.pallas_call(
        functools.partial(kernel, sizes),
        out_shape=(jax.ShapeDtypeStruct((3, 256), F32), jax.ShapeDtypeStruct((4, 128), F32)),
        in_specs=[pl.BlockSpec(memory_space=pltpu.HBM)] * 6,
        out_specs=(vmem, vmem),
        scratch_shapes=[
            pltpu.VMEM((4, 128), F32),
            pltpu.VMEM((3, 256), jnp.int32),
            pltpu.VMEM((3, ng * 512), jnp.int32),
            pltpu.VMEM((1, SLOTS), jnp.int32),
            pltpu.VMEM((1, SLOTS), jnp.int32),
            pltpu.VMEM((1, 1), jnp.int32),
            pltpu.VMEM((8, 128), jnp.int32),
            pltpu.SMEM((8, 128), jnp.int32),
            pltpu.VMEM((3, 4 * ng, 128), F32),
            pltpu.VMEM((SLOTS, 3, GROUPS, 2, 8, 128), F32),
            pltpu.VMEM((4, 3, GROUPS, 8, 128), F32),
            pltpu.VMEM((SLOTS, 24, 8, 128), F32),
            pltpu.VMEM((4 * ng, 384), jnp.bfloat16),
            pltpu.VMEM((3, 256, 128), F32),
            pltpu.VMEM((128, 128), F32),
            pltpu.VMEM((4 * ng, 128), F32),
            pltpu.VMEM((4 * ng, 128), F32),
            pltpu.VMEM((4 * ng, 128), F32),
            pltpu.VMEM((ITERS, 4, 128), F32),
            pltpu.VMEM((ITERS, ng, 4, 128), F32),
            pltpu.VMEM((ITERS, ng, 4, 128), F32),
            pltpu.VMEM((ITERS, ng - 1, 4, 128), F32),
            pltpu.VMEM((ITERS, 8, 128), F32),
            pltpu.VMEM((ITERS, npl, 8, 128), F32),
            pltpu.VMEM((1, 128), F32),
            pltpu.VMEM((npl, 1, 128), F32),
            pltpu.VMEM((1, 128), F32),
            pltpu.VMEM((ng, 1, 128), F32),
            pltpu.SemaphoreType.DMA((2, ITERS)),
            pltpu.SemaphoreType.DMA((2, ITERS)),
            pltpu.SemaphoreType.DMA((ITERS, 2)),
            pltpu.SemaphoreType.DMA((2,)),
            pltpu.SemaphoreType.DMA((2,)),
            pltpu.SemaphoreType.DMA((7,)),
        ],
        compiler_params=pltpu.CompilerParams(collective_id=1, has_side_effects=True, vmem_limit_bytes=60 << 20),
        name="solve",
    )(field.reshape(4, 128), grain_positions, pixel_coords, block_grain, block_pixel, block_count)
    held = pl.BlockSpec(memory_space=pltpu.HBM)
    moments, residual = pl.pallas_call(
        hand_on,
        out_shape=(jax.ShapeDtypeStruct((3, 256), F32), jax.ShapeDtypeStruct((4, 128), F32)),
        in_specs=[held] * 2,
        out_specs=(held, held),
        scratch_shapes=[pltpu.SemaphoreType.DMA((2,))],
        compiler_params=pltpu.CompilerParams(vmem_limit_bytes=60 << 20),
        name="hand_on",
    )(moments, residual)
    return moments, residual.reshape(512)


def solution(mesh, rows=4):
    grain, plane = mesh.shape["grain"], mesh.shape["plane"]
    placed = (
        P(("plane", "grain")),
        P(None, "grain"),
        P(None, "plane"),
        P("plane", "grain"),
        P("plane", "grain"),
        P("plane", "grain"),
    )
    return jax.shard_map(
        functools.partial(local, (rows, grain // rows, plane)),
        mesh=mesh,
        in_specs=placed,
        out_specs=(P(None, "grain"), P(("plane", "grain"))),
        check_vma=False,
    )
```

```python
import functools

import jax
import jax.numpy as jnp
from jax import lax
from jax.experimental import pallas as pl
from jax.experimental.pallas import tpu as pltpu
from jax.sharding import PartitionSpec as P

MESH = pl.DeviceIdType.MESH
BLOCK_G = 64
ITERS = 3
SLOTS = 36
UNROLL = 6
GROUPS = 8
F32 = jnp.float32


def kernel(
    sizes,
    field_in,
    grains_in,
    pixels_in,
    block_grain_in,
    block_pixel_in,
    block_count_in,
    moments_out,
    residual_out,
    field,
    grains,
    pixels,
    block_grain,
    block_pixel,
    block_count,
    table_made,
    table,
    coords,
    sens,
    spread,
    snap,
    picks,
    unfold,
    contrib,
    rows,
    full_residual,
    full_image,
    gather_send,
    gathered,
    part_send,
    part_recv,
    grad_send,
    grad_recv,
    norm_send,
    norm_recv,
    total_send,
    total_recv,
    gather_sem,
    part_sem,
    grad_sem,
    last_sem,
    total_sem,
    local_sem,
):
    nx, nz, npl = sizes
    ng = nx * nz
    far = nz // 2
    g, p = lax.axis_index("grain"), lax.axis_index("plane")
    x, z = g // nz, lax.rem(g, nz)

    columns = [lax.rem(x + a, nx) * nz for a in range(nx)]
    across = sorted(range(nx), key=lambda a: -min(a, nx - a))

    def grain_peers(body):
        def far_row(m, carry):
            d = far + (1 - 2 * lax.rem(m, 2)) * ((m + 1) // 2)
            row = lax.rem(z + d, nz)
            for a in across:
                body(m * nx + a, columns[a] + row)
            return carry

        lax.fori_loop(0, nz - 1, far_row, 0)
        for a in across[:-1]:
            body((nz - 1) * nx + a - 1, columns[a] + z)

    def plane_peers(body):
        for i in range(1, npl):
            body(lax.rem(p + i, npl))

    def each(n, body):
        def step(i, carry):
            body(i)
            return carry

        lax.fori_loop(0, n, step, 0)

    def to_grains(source, place, send_sem, recv_sem):
        def send(i, peer):
            pltpu.make_async_remote_copy(
                src_ref=source(peer),
                dst_ref=place(i),
                send_sem=send_sem,
                recv_sem=recv_sem,
                device_id=(peer, p),
                device_id_type=MESH,
            ).start()

        grain_peers(send)

    def plane_sum(value, sent, landed, sems):
        sent[...] = value

        def send(peer):
            pltpu.make_async_remote_copy(
                src_ref=sent,
                dst_ref=landed.at[p],
                send_sem=sems.at[0],
                recv_sem=sems.at[1],
                device_id=(g, peer),
                device_id_type=MESH,
            ).start()

        plane_peers(send)
        landed[p] = value
        wait(landed.at[pl.ds(0, npl - 1)], sems.at[1])
        return jnp.sum(landed[...], axis=0)

    def wait(ref, sem):
        pltpu.make_async_copy(ref, ref, sem).wait()

    barrier = pltpu.get_barrier_semaphore()
    grain_peers(lambda i, peer: pl.semaphore_signal(barrier, inc=1, device_id=(peer, p), device_id_type=MESH))
    plane_peers(lambda peer: pl.semaphore_signal(barrier, inc=1, device_id=(g, peer), device_id_type=MESH))
    loads = [
        pltpu.make_async_copy(src, dst, local_sem.at[i])
        for i, (src, dst) in enumerate(
            [
                (block_grain_in, block_grain),
                (block_pixel_in, block_pixel),
                (block_count_in, block_count),
                (grains_in, grains),
                (pixels_in, pixels),
                (field_in, field),
            ]
        )
    ]
    for load in loads:
        load.start()
    for load in loads:
        load.wait()

    lane = lax.broadcasted_iota(jnp.int32, (8, 128), 1)

    def broadcast_lanes(tile):
        for r in range(96):
            c, b, k = r // 32, r // 8 % 4, r % 8
            spread[b, c, k] = jnp.broadcast_to(tile[:, r : r + 1], (8, 128))

    sub, col = (lax.broadcasted_iota(jnp.int32, (40, 128), i) for i in range(2))
    slot = jnp.where(col < 64, col, col - 64)
    row = lax.broadcasted_iota(jnp.int32, (1, 128), 1)
    edge = lax.broadcasted_iota(jnp.int32, (1, SLOTS), 1)
    count = block_count[...]

    def wide(value, fill):
        return jnp.concatenate([value, jnp.full((1, 128 - SLOTS), fill, jnp.int32)], axis=1)

    def upright(value):
        return jnp.sum(jnp.where(sub == col, value, 0), axis=1, keepdims=True)

    def over_slots(value):
        return jnp.sum(value, axis=0, keepdims=True)

    key = wide(jnp.where(edge < count, block_grain[...], 4), 5)
    key_up = upright(key)
    real = sub[:, 0:1] < SLOTS
    ahead = (key < key_up) | ((key == key_up) & (col < sub))
    rank = jnp.sum(ahead.astype(jnp.int32), axis=1, keepdims=True)
    place = (rank == slot) & real
    pixel = over_slots(jnp.where(place, upright(wide(block_pixel[...], 0)), 0))
    block = over_slots(jnp.where(place, key_up, 0))
    alive = over_slots(jnp.where(place & (key_up < 4), 1, 0))
    block = jnp.minimum(block, 3)
    below = over_slots(jnp.where((key_up < block) & real, 1, 0))
    same = jnp.where((row > 0) & ((row > below) | (alive == 0)), 1, 0)
    upto = over_slots(jnp.where((key_up <= row) & real, 1, 0))
    held = over_slots(jnp.where((key_up == row) & real, 1, 0))
    zero = jnp.zeros((1, 128), jnp.int32)
    table_made[...] = jnp.concatenate(
        [pixel, block, alive, same, jnp.maximum(upto - 1, 0), jnp.minimum(held, 1), zero, zero], axis=0
    )
    to_scalars = pltpu.make_async_copy(table_made, table, local_sem.at[6])
    to_scalars.start()
    target = jnp.where(alive > 0, 2 * pixel + jnp.where(row < 64, 0, 1), -1)
    chosen = (lax.broadcasted_iota(jnp.int32, (4 * ng, 128), 0) == target).astype(F32).astype(jnp.bfloat16)
    for i in range(3):
        picks[:, 128 * i : 128 * (i + 1)] = chosen

    grain_s = lax.broadcasted_iota(jnp.int32, (8, 256), 0) == lax.rem(lax.broadcasted_iota(jnp.int32, (8, 256), 1), 8)

    def product(a, b, over):
        return lax.dot_general(
            a, b, (((1,), (over,)), ((), ())), precision=lax.Precision.HIGHEST, preferred_element_type=F32
        )

    for c in range(3):
        eighth = lax.broadcasted_iota(jnp.int32, (256, 128), 0) // 8
        unfold[c] = (eighth + 32 * c == lax.broadcasted_iota(jnp.int32, (256, 128), 1)).astype(F32)

    def to_tile(value):
        return sum(product(jnp.where(grain_s, value[c : c + 1, :], 0.0), unfold[c], 0) for c in range(3))

    def from_tile(tile):
        parts = [jnp.sum(jnp.where(grain_s, product(tile, unfold[c], 1), 0.0), axis=0, keepdims=True) for c in range(3)]
        return jnp.concatenate(parts, axis=0)

    broadcast_lanes(to_tile(grains[...].astype(F32) * 0.03125))
    contrib[...] = jnp.zeros((128, 128), F32)

    for c in range(3):
        coords[c] = (pixels[c : c + 1, :].astype(F32) * 0.03125).reshape(4 * ng, 128)

    def make_sens(j):
        e, b = table[0, j], table[1, j]
        scale = table[2, j].astype(F32) * 27.0
        for h in range(2):
            px, py, pz = (coords[c, pl.ds(2 * e + h, 1), :] for c in range(3))
            for k in range(GROUPS):
                dx = px - spread[b, 0, k]
                dy = py - spread[b, 1, k]
                dz = pz - spread[b, 2, k]
                inv = lax.rsqrt(dx * dx + dy * dy + dz * dz)
                inv2 = inv * inv
                inv3 = inv2 * inv * scale
                along = 3.0 * dz * inv2 * inv3
                sens[j, 0, k, h] = along * dx
                sens[j, 1, k, h] = along * dy
                sens[j, 2, k, h] = along * dz - inv3

    def gather(it):
        to_grains(lambda peer: gather_send.at[it], lambda i: gathered.at[it, g], gather_sem.at[0, it], gather_sem.at[1, it])
        gathered[it, g] = gather_send[it]

    def gather_wait(it):
        wait(gathered.at[it, pl.ds(0, ng - 1)], gather_sem.at[1, it])

    def pairwise(values):
        while len(values) > 1:
            values = [sum(values[i : i + 2]) for i in range(0, len(values), 2)]
        return values[0]

    def unrolled(step):
        def several(i, carry):
            for u in range(UNROLL):
                carry = step(i * UNROLL + u, carry)
            return carry

        return several

    def backward():
        def step(j, acc):
            e = table[0, j]
            keep = table[3, j].astype(F32)
            v0 = jnp.broadcast_to(rows[pl.ds(2 * e, 1), :], (8, 128))
            v1 = jnp.broadcast_to(rows[pl.ds(2 * e + 1, 1), :], (8, 128))
            out = []
            for c in range(3):
                for k in range(GROUPS):
                    i = c * GROUPS + k
                    t = acc[i] * keep + (sens[j, c, k, 0] * v0 + sens[j, c, k, 1] * v1)
                    snap[j, i] = t
                    out.append(t)
            return tuple(out)

        lax.fori_loop(0, SLOTS // UNROLL, unrolled(step), tuple(jnp.zeros((8, 128), F32) for _ in range(24)))
        totals = []
        for b in range(4):
            last = table[4, b]
            held = table[5, b].astype(F32)
            for c in range(3):
                part = jnp.zeros((8, 128), F32)
                for k in range(GROUPS):
                    s = jnp.sum(snap[last, c * GROUPS + k], axis=1, keepdims=True)
                    part = jnp.where(lane == c * 32 + b * 8 + k, s, part)
                totals.append(part * held)
        return pairwise(totals)

    def forward(it, meanwhile):
        def step(j, carry):
            b = table[1, j]
            acc = [[jnp.zeros((8, 128), F32) for _ in range(2)] for _ in range(2)]
            for c in range(3):
                for k in range(GROUPS):
                    d = spread[b, c, k]
                    for h in range(2):
                        acc[h][k % 2] = acc[h][k % 2] + sens[j, c, k, h] * d
            for h in range(2):
                contrib[pl.ds(64 * h + j, 1), :] = jnp.sum(acc[h][0] + acc[h][1], axis=0, keepdims=True)
            return carry

        lax.fori_loop(0, SLOTS // UNROLL, unrolled(step), 0)
        value = contrib[...]
        high = value.astype(jnp.bfloat16)
        rest = value - high.astype(F32)
        middle = rest.astype(jnp.bfloat16)
        low = (rest - middle.astype(F32)).astype(jnp.bfloat16)
        pieces = jnp.concatenate([high, middle, low], axis=0)
        part = jnp.dot(picks[...], pieces, preferred_element_type=F32)
        part_send[it] = part.reshape(ng, 4, 128)
        to_grains(lambda peer: part_send.at[it, peer], lambda i: part_recv.at[it, i], part_sem.at[0, it], part_sem.at[1, it])
        meanwhile()
        wait(part_recv.at[it], part_sem.at[1, it])
        chains = [jnp.sum(part_recv[it, i : min(i + 8, ng - 1)], axis=0) for i in range(0, ng - 1, 8)]
        return pairwise(chains) + part_send[it, g]

    def grad_sum(it, tile):
        return plane_sum(tile, grad_send.at[it], grad_recv.at[it], grad_sem.at[it])

    def column(value):
        return jnp.sum(jnp.sum(value.reshape(-1, 8, 128), axis=0), axis=1, keepdims=True)

    def full_sum(value):
        return jnp.sum(jnp.sum(value, axis=0, keepdims=True), axis=1, keepdims=True)

    to_scalars.wait()
    gather_send[0] = field[...]
    pl.semaphore_wait(barrier, ng - 1 + npl - 1)
    gather(0)
    each(SLOTS, make_sens)
    gather_wait(0)
    rows[...] = gathered[0].reshape(4 * ng, 128)
    full_residual[...] = rows[...]

    grad = grad_sum(0, backward())
    residual = field[...]
    moments = direction = pull = jnp.zeros((8, 128), F32)
    image = jnp.zeros((4, 128), F32)
    gamma = jnp.ones((1, 1), F32)
    alpha = beta = delta = jnp.zeros((1, 1), F32)
    full_image[...] = jnp.zeros((4 * ng, 128), F32)
    for it in range(ITERS):
        broadcast_lanes(grad)

        def meanwhile():
            if 0 < it < ITERS - 1:
                full_image[...] = rows[...] + beta * full_image[...]
                full_residual[...] = full_residual[...] - alpha * full_image[...]

        push = forward(it, meanwhile)
        if it + 1 < ITERS:
            gather_send[it + 1] = push
            gather(it + 1)
            gather_wait(it + 1)
            full = gathered[it + 1].reshape(4 * ng, 128)
            rows[...] = full
            sums = [column(full_residual[...] * full), column(full * full), column(full * full_image[...])]
            tile = backward()
            for i, value in enumerate(sums):
                tile = jnp.where(lane == 96 + i, value, tile)
            tile = grad_sum(it + 1, tile)
            totals = jnp.sum(tile, axis=0, keepdims=True)
            gamma_new = totals[:, 96:97]
            beta = gamma_new / gamma if it > 0 else jnp.zeros((1, 1), F32)
            delta = totals[:, 97:98] + 2.0 * beta * totals[:, 98:99] + beta * beta * delta
            gamma = gamma_new
            alpha = gamma / delta
            pull = jnp.where(lane >= 96, 0.0, tile) + beta * pull
            direction = grad + beta * direction
            moments = moments + alpha * direction
            image = push + beta * image
            residual = residual - alpha * image
            grad = grad - alpha * pull
        else:
            spot = lax.broadcasted_iota(jnp.int32, (1, 128), 1)
            sums = jnp.zeros((1, 128), F32)
            for i, other in enumerate((residual, push, image)):
                sums = jnp.where(spot == i, full_sum(push * other), sums)
            sums = plane_sum(sums, norm_send, norm_recv, last_sem)
            total_send[...] = sums
            total_recv[g] = sums
            to_grains(lambda peer: total_send, lambda i: total_recv.at[g], total_sem.at[0], total_sem.at[1])
            moments_flat, direction_flat, grad_flat = from_tile(moments), from_tile(direction), from_tile(grad)
            wait(total_recv.at[pl.ds(0, ng - 1)], total_sem.at[1])
            sums = pairwise([jnp.sum(total_recv[i : i + 8], axis=0) for i in range(0, ng, 8)])
            beta = sums[:, 0:1] / gamma
            delta = sums[:, 1:2] + 2.0 * beta * sums[:, 2:3] + beta * beta * delta
            alpha = sums[:, 0:1] / delta
            moments_out[...] = moments_flat + alpha * (grad_flat + beta * direction_flat)
            residual_out[...] = residual - alpha * (push + beta * image)

    for it in range(ITERS):
        wait(gathered.at[it, pl.ds(0, ng - 1)], gather_sem.at[0, it])
        wait(part_recv.at[it], part_sem.at[0, it])
        wait(grad_recv.at[it, pl.ds(0, npl - 1)], grad_sem.at[it, 0])
    wait(norm_recv.at[pl.ds(0, npl - 1)], last_sem.at[0])
    wait(total_recv.at[pl.ds(0, ng - 1)], total_sem.at[0])


def hand_on(moments, residual, moments_out, residual_out, sems):
    copies = [
        pltpu.make_async_copy(moments, moments_out, sems.at[0]),
        pltpu.make_async_copy(residual, residual_out, sems.at[1]),
    ]
    for copy in copies:
        copy.start()
    for copy in copies:
        copy.wait()


def local(sizes, field, grain_positions, pixel_coords, block_grain, block_pixel, block_count):
    nx, nz, npl = sizes
    ng = nx * nz
    vmem = pl.BlockSpec(memory_space=pltpu.VMEM)
    moments, residual = pl.pallas_call(
        functools.partial(kernel, sizes),
        out_shape=(jax.ShapeDtypeStruct((3, 256), F32), jax.ShapeDtypeStruct((4, 128), F32)),
        in_specs=[pl.BlockSpec(memory_space=pltpu.HBM)] * 6,
        out_specs=(vmem, vmem),
        scratch_shapes=[
            pltpu.VMEM((4, 128), F32),
            pltpu.VMEM((3, 256), jnp.int32),
            pltpu.VMEM((3, ng * 512), jnp.int32),
            pltpu.VMEM((1, SLOTS), jnp.int32),
            pltpu.VMEM((1, SLOTS), jnp.int32),
            pltpu.VMEM((1, 1), jnp.int32),
            pltpu.VMEM((8, 128), jnp.int32),
            pltpu.SMEM((8, 128), jnp.int32),
            pltpu.VMEM((3, 4 * ng, 128), F32),
            pltpu.VMEM((SLOTS, 3, GROUPS, 2, 8, 128), F32),
            pltpu.VMEM((4, 3, GROUPS, 8, 128), F32),
            pltpu.VMEM((SLOTS, 24, 8, 128), F32),
            pltpu.VMEM((4 * ng, 384), jnp.bfloat16),
            pltpu.VMEM((3, 256, 128), F32),
            pltpu.VMEM((128, 128), F32),
            pltpu.VMEM((4 * ng, 128), F32),
            pltpu.VMEM((4 * ng, 128), F32),
            pltpu.VMEM((4 * ng, 128), F32),
            pltpu.VMEM((ITERS, 4, 128), F32),
            pltpu.VMEM((ITERS, ng, 4, 128), F32),
            pltpu.VMEM((ITERS, ng, 4, 128), F32),
            pltpu.VMEM((ITERS, ng - 1, 4, 128), F32),
            pltpu.VMEM((ITERS, 8, 128), F32),
            pltpu.VMEM((ITERS, npl, 8, 128), F32),
            pltpu.VMEM((1, 128), F32),
            pltpu.VMEM((npl, 1, 128), F32),
            pltpu.VMEM((1, 128), F32),
            pltpu.VMEM((ng, 1, 128), F32),
            pltpu.SemaphoreType.DMA((2, ITERS)),
            pltpu.SemaphoreType.DMA((2, ITERS)),
            pltpu.SemaphoreType.DMA((ITERS, 2)),
            pltpu.SemaphoreType.DMA((2,)),
            pltpu.SemaphoreType.DMA((2,)),
            pltpu.SemaphoreType.DMA((7,)),
        ],
        compiler_params=pltpu.CompilerParams(collective_id=1, has_side_effects=True, vmem_limit_bytes=40 << 20),
        name="solve",
    )(
        *(
            pltpu.with_memory_space_constraint(value, pltpu.HBM)
            for value in (field.reshape(4, 128), grain_positions, pixel_coords, block_grain, block_pixel)
        ),
        block_count,
    )
    held = pl.BlockSpec(memory_space=pltpu.HBM)
    moments, residual = pl.pallas_call(
        hand_on,
        out_shape=(jax.ShapeDtypeStruct((3, 256), F32), jax.ShapeDtypeStruct((4, 128), F32)),
        in_specs=[vmem] * 2,
        out_specs=(held, held),
        scratch_shapes=[pltpu.SemaphoreType.DMA((2,))],
        compiler_params=pltpu.CompilerParams(vmem_limit_bytes=40 << 20),
        name="hand_on",
    )(moments, residual)
    return moments, residual.reshape(512)


def solution(mesh, rows=4):
    grain, plane = mesh.shape["grain"], mesh.shape["plane"]
    placed = (
        P(("plane", "grain")),
        P(None, "grain"),
        P(None, "plane"),
        P("plane", "grain"),
        P("plane", "grain"),
        P("plane", "grain"),
    )
    return jax.shard_map(
        functools.partial(local, (rows, grain // rows, plane)),
        mesh=mesh,
        in_specs=placed,
        out_specs=(P(None, "grain"), P(("plane", "grain"))),
        check_vma=False,
    )
```

```python
import functools

import jax
import jax.numpy as jnp
from jax import lax
from jax.experimental import pallas as pl
from jax.experimental.pallas import tpu as pltpu
from jax.sharding import PartitionSpec as P

MESH = pl.DeviceIdType.MESH
BLOCK_G = 64
ITERS = 3
SLOTS = 36
UNROLL = 12
GROUPS = 8
F32 = jnp.float32


def kernel(
    sizes,
    field_in,
    grains_in,
    pixels_in,
    block_grain_in,
    block_pixel_in,
    block_count_in,
    moments_out,
    residual_out,
    field,
    grains,
    pixels,
    block_grain,
    block_pixel,
    block_count,
    table_made,
    table,
    coords,
    sens,
    spread,
    snap,
    picks,
    unfold,
    contrib,
    rows,
    full_residual,
    full_image,
    gather_send,
    gathered,
    part_send,
    part_recv,
    grad_send,
    grad_recv,
    norm_send,
    norm_recv,
    total_send,
    total_recv,
    gather_sem,
    part_sem,
    grad_sem,
    last_sem,
    total_sem,
    local_sem,
):
    nx, nz, npl = sizes
    ng = nx * nz
    far = nz // 2
    g, p = lax.axis_index("grain"), lax.axis_index("plane")
    x, z = g // nz, lax.rem(g, nz)

    columns = [lax.rem(x + a, nx) * nz for a in range(nx)]
    across = sorted(range(nx), key=lambda a: -min(a, nx - a))

    def grain_peers(body):
        def far_row(m, carry):
            d = far + (1 - 2 * lax.rem(m, 2)) * ((m + 1) // 2)
            row = lax.rem(z + d, nz)
            for a in across:
                body(m * nx + a, columns[a] + row)
            return carry

        lax.fori_loop(0, nz - 1, far_row, 0)
        for a in across[:-1]:
            body((nz - 1) * nx + a - 1, columns[a] + z)

    def plane_peers(body):
        for i in range(1, npl):
            body(lax.rem(p + i, npl))

    def each(n, body):
        def step(i, carry):
            body(i)
            return carry

        lax.fori_loop(0, n, step, 0)

    def to_grains(source, place, send_sem, recv_sem):
        def send(i, peer):
            pltpu.make_async_remote_copy(
                src_ref=source(peer),
                dst_ref=place(i),
                send_sem=send_sem,
                recv_sem=recv_sem,
                device_id=(peer, p),
                device_id_type=MESH,
            ).start()

        grain_peers(send)

    def plane_sum(value, sent, landed, sems):
        sent[...] = value

        def send(peer):
            pltpu.make_async_remote_copy(
                src_ref=sent,
                dst_ref=landed.at[p],
                send_sem=sems.at[0],
                recv_sem=sems.at[1],
                device_id=(g, peer),
                device_id_type=MESH,
            ).start()

        plane_peers(send)
        landed[p] = value
        wait(landed.at[pl.ds(0, npl - 1)], sems.at[1])
        return jnp.sum(landed[...], axis=0)

    def wait(ref, sem):
        pltpu.make_async_copy(ref, ref, sem).wait()

    barrier = pltpu.get_barrier_semaphore()
    grain_peers(lambda i, peer: pl.semaphore_signal(barrier, inc=1, device_id=(peer, p), device_id_type=MESH))
    plane_peers(lambda peer: pl.semaphore_signal(barrier, inc=1, device_id=(g, peer), device_id_type=MESH))
    loads = [
        pltpu.make_async_copy(src, dst, local_sem.at[i])
        for i, (src, dst) in enumerate(
            [
                (block_grain_in, block_grain),
                (block_pixel_in, block_pixel),
                (block_count_in, block_count),
                (grains_in, grains),
                (pixels_in, pixels),
                (field_in, field),
            ]
        )
    ]
    for load in loads:
        load.start()
    for load in loads:
        load.wait()

    lane = lax.broadcasted_iota(jnp.int32, (8, 128), 1)

    def broadcast_lanes(tile):
        for r in range(96):
            c, b, k = r // 32, r // 8 % 4, r % 8
            spread[b, c, k] = jnp.broadcast_to(tile[:, r : r + 1], (8, 128))

    sub, col = (lax.broadcasted_iota(jnp.int32, (40, 128), i) for i in range(2))
    slot = jnp.where(col < 64, col, col - 64)
    row = lax.broadcasted_iota(jnp.int32, (1, 128), 1)
    edge = lax.broadcasted_iota(jnp.int32, (1, SLOTS), 1)
    count = block_count[...]

    def wide(value, fill):
        return jnp.concatenate([value, jnp.full((1, 128 - SLOTS), fill, jnp.int32)], axis=1)

    def upright(value):
        return jnp.sum(jnp.where(sub == col, value, 0), axis=1, keepdims=True)

    def over_slots(value):
        return jnp.sum(value, axis=0, keepdims=True)

    key = wide(jnp.where(edge < count, block_grain[...], 4), 5)
    key_up = upright(key)
    real = sub[:, 0:1] < SLOTS
    ahead = (key < key_up) | ((key == key_up) & (col < sub))
    rank = jnp.sum(ahead.astype(jnp.int32), axis=1, keepdims=True)
    place = (rank == slot) & real
    pixel = over_slots(jnp.where(place, upright(wide(block_pixel[...], 0)), 0))
    block = over_slots(jnp.where(place, key_up, 0))
    alive = over_slots(jnp.where(place & (key_up < 4), 1, 0))
    block = jnp.minimum(block, 3)
    below = over_slots(jnp.where((key_up < block) & real, 1, 0))
    same = jnp.where((row > 0) & ((row > below) | (alive == 0)), 1, 0)
    upto = over_slots(jnp.where((key_up <= row) & real, 1, 0))
    held = over_slots(jnp.where((key_up == row) & real, 1, 0))
    zero = jnp.zeros((1, 128), jnp.int32)
    table_made[...] = jnp.concatenate(
        [pixel, block, alive, same, jnp.maximum(upto - 1, 0), jnp.minimum(held, 1), zero, zero], axis=0
    )
    to_scalars = pltpu.make_async_copy(table_made, table, local_sem.at[6])
    to_scalars.start()
    target = jnp.where(alive > 0, 2 * pixel + jnp.where(row < 64, 0, 1), -1)
    chosen = (lax.broadcasted_iota(jnp.int32, (4 * ng, 128), 0) == target).astype(F32).astype(jnp.bfloat16)
    for i in range(3):
        picks[:, 128 * i : 128 * (i + 1)] = chosen

    grain_s = lax.broadcasted_iota(jnp.int32, (8, 256), 0) == lax.rem(lax.broadcasted_iota(jnp.int32, (8, 256), 1), 8)

    def product(a, b, over):
        return lax.dot_general(
            a, b, (((1,), (over,)), ((), ())), precision=lax.Precision.HIGHEST, preferred_element_type=F32
        )

    for c in range(3):
        eighth = lax.broadcasted_iota(jnp.int32, (256, 128), 0) // 8
        unfold[c] = (eighth + 32 * c == lax.broadcasted_iota(jnp.int32, (256, 128), 1)).astype(F32)

    def to_tile(value):
        return sum(product(jnp.where(grain_s, value[c : c + 1, :], 0.0), unfold[c], 0) for c in range(3))

    def from_tile(tile):
        parts = [jnp.sum(jnp.where(grain_s, product(tile, unfold[c], 1), 0.0), axis=0, keepdims=True) for c in range(3)]
        return jnp.concatenate(parts, axis=0)

    broadcast_lanes(to_tile(grains[...].astype(F32) * 0.03125))
    contrib[...] = jnp.zeros((128, 128), F32)

    for c in range(3):
        coords[c] = (pixels[c : c + 1, :].astype(F32) * 0.03125).reshape(4 * ng, 128)

    def make_sens(j):
        e, b = table[0, j], table[1, j]
        scale = table[2, j].astype(F32) * 27.0
        for h in range(2):
            px, py, pz = (coords[c, pl.ds(2 * e + h, 1), :] for c in range(3))
            for k in range(GROUPS):
                dx = px - spread[b, 0, k]
                dy = py - spread[b, 1, k]
                dz = pz - spread[b, 2, k]
                inv = lax.rsqrt(dx * dx + dy * dy + dz * dz)
                inv2 = inv * inv
                inv3 = inv2 * inv * scale
                along = 3.0 * dz * inv2 * inv3
                sens[j, 0, k, h] = along * dx
                sens[j, 1, k, h] = along * dy
                sens[j, 2, k, h] = along * dz - inv3

    def gather(it):
        to_grains(lambda peer: gather_send.at[it], lambda i: gathered.at[it, g], gather_sem.at[0, it], gather_sem.at[1, it])
        gathered[it, g] = gather_send[it]

    def gather_wait(it):
        wait(gathered.at[it, pl.ds(0, ng - 1)], gather_sem.at[1, it])

    def pairwise(values):
        while len(values) > 1:
            values = [sum(values[i : i + 2]) for i in range(0, len(values), 2)]
        return values[0]

    def unrolled(step):
        def several(i, carry):
            for u in range(UNROLL):
                carry = step(i * UNROLL + u, carry)
            return carry

        return several

    def backward():
        def step(j, acc):
            e = table[0, j]
            keep = table[3, j].astype(F32)
            v0 = jnp.broadcast_to(rows[pl.ds(2 * e, 1), :], (8, 128))
            v1 = jnp.broadcast_to(rows[pl.ds(2 * e + 1, 1), :], (8, 128))
            out = []
            for c in range(3):
                for k in range(GROUPS):
                    i = c * GROUPS + k
                    t = acc[i] * keep + (sens[j, c, k, 0] * v0 + sens[j, c, k, 1] * v1)
                    snap[j, i] = t
                    out.append(t)
            return tuple(out)

        lax.fori_loop(0, SLOTS // UNROLL, unrolled(step), tuple(jnp.zeros((8, 128), F32) for _ in range(24)))
        totals = []
        for b in range(4):
            last = table[4, b]
            held = table[5, b].astype(F32)
            for c in range(3):
                part = jnp.zeros((8, 128), F32)
                for k in range(GROUPS):
                    s = jnp.sum(snap[last, c * GROUPS + k], axis=1, keepdims=True)
                    part = jnp.where(lane == c * 32 + b * 8 + k, s, part)
                totals.append(part * held)
        return pairwise(totals)

    def forward(it, meanwhile):
        def step(j, carry):
            b = table[1, j]
            acc = [[jnp.zeros((8, 128), F32) for _ in range(2)] for _ in range(2)]
            for c in range(3):
                for k in range(GROUPS):
                    d = spread[b, c, k]
                    for h in range(2):
                        acc[h][k % 2] = acc[h][k % 2] + sens[j, c, k, h] * d
            for h in range(2):
                contrib[pl.ds(64 * h + j, 1), :] = jnp.sum(acc[h][0] + acc[h][1], axis=0, keepdims=True)
            return carry

        lax.fori_loop(0, SLOTS // UNROLL, unrolled(step), 0)
        value = contrib[...]
        high = value.astype(jnp.bfloat16)
        rest = value - high.astype(F32)
        middle = rest.astype(jnp.bfloat16)
        low = (rest - middle.astype(F32)).astype(jnp.bfloat16)
        pieces = jnp.concatenate([high, middle, low], axis=0)
        part = jnp.dot(picks[...], pieces, preferred_element_type=F32)
        part_send[it] = part.reshape(ng, 4, 128)
        to_grains(lambda peer: part_send.at[it, peer], lambda i: part_recv.at[it, i], part_sem.at[0, it], part_sem.at[1, it])
        meanwhile()
        wait(part_recv.at[it], part_sem.at[1, it])
        chains = [jnp.sum(part_recv[it, i : min(i + 8, ng - 1)], axis=0) for i in range(0, ng - 1, 8)]
        return pairwise(chains) + part_send[it, g]

    def grad_sum(it, tile):
        return plane_sum(tile, grad_send.at[it], grad_recv.at[it], grad_sem.at[it])

    def column(value):
        return jnp.sum(jnp.sum(value.reshape(-1, 8, 128), axis=0), axis=1, keepdims=True)

    def full_sum(value):
        return jnp.sum(jnp.sum(value, axis=0, keepdims=True), axis=1, keepdims=True)

    to_scalars.wait()
    gather_send[0] = field[...]
    pl.semaphore_wait(barrier, ng - 1 + npl - 1)
    gather(0)
    each(SLOTS, make_sens)
    gather_wait(0)
    rows[...] = gathered[0].reshape(4 * ng, 128)
    full_residual[...] = rows[...]

    grad = grad_sum(0, backward())
    residual = field[...]
    moments = direction = pull = jnp.zeros((8, 128), F32)
    image = jnp.zeros((4, 128), F32)
    gamma = jnp.ones((1, 1), F32)
    alpha = beta = delta = jnp.zeros((1, 1), F32)
    full_image[...] = jnp.zeros((4 * ng, 128), F32)
    for it in range(ITERS):
        broadcast_lanes(grad)

        def meanwhile():
            if 0 < it < ITERS - 1:
                full_image[...] = rows[...] + beta * full_image[...]
                full_residual[...] = full_residual[...] - alpha * full_image[...]

        push = forward(it, meanwhile)
        if it + 1 < ITERS:
            gather_send[it + 1] = push
            gather(it + 1)
            gather_wait(it + 1)
            full = gathered[it + 1].reshape(4 * ng, 128)
            rows[...] = full
            sums = [column(full_residual[...] * full), column(full * full), column(full * full_image[...])]
            tile = backward()
            for i, value in enumerate(sums):
                tile = jnp.where(lane == 96 + i, value, tile)
            tile = grad_sum(it + 1, tile)
            totals = jnp.sum(tile, axis=0, keepdims=True)
            gamma_new = totals[:, 96:97]
            beta = gamma_new / gamma if it > 0 else jnp.zeros((1, 1), F32)
            delta = totals[:, 97:98] + 2.0 * beta * totals[:, 98:99] + beta * beta * delta
            gamma = gamma_new
            alpha = gamma / delta
            pull = jnp.where(lane >= 96, 0.0, tile) + beta * pull
            direction = grad + beta * direction
            moments = moments + alpha * direction
            image = push + beta * image
            residual = residual - alpha * image
            grad = grad - alpha * pull
        else:
            spot = lax.broadcasted_iota(jnp.int32, (1, 128), 1)
            sums = jnp.zeros((1, 128), F32)
            for i, other in enumerate((residual, push, image)):
                sums = jnp.where(spot == i, full_sum(push * other), sums)
            sums = plane_sum(sums, norm_send, norm_recv, last_sem)
            total_send[...] = sums
            total_recv[g] = sums
            to_grains(lambda peer: total_send, lambda i: total_recv.at[g], total_sem.at[0], total_sem.at[1])
            moments_flat, direction_flat, grad_flat = from_tile(moments), from_tile(direction), from_tile(grad)
            wait(total_recv.at[pl.ds(0, ng - 1)], total_sem.at[1])
            sums = pairwise([jnp.sum(total_recv[i : i + 8], axis=0) for i in range(0, ng, 8)])
            beta = sums[:, 0:1] / gamma
            delta = sums[:, 1:2] + 2.0 * beta * sums[:, 2:3] + beta * beta * delta
            alpha = sums[:, 0:1] / delta
            moments_out[...] = moments_flat + alpha * (grad_flat + beta * direction_flat)
            residual_out[...] = residual - alpha * (push + beta * image)

    for it in range(ITERS):
        wait(gathered.at[it, pl.ds(0, ng - 1)], gather_sem.at[0, it])
        wait(part_recv.at[it], part_sem.at[0, it])
        wait(grad_recv.at[it, pl.ds(0, npl - 1)], grad_sem.at[it, 0])
    wait(norm_recv.at[pl.ds(0, npl - 1)], last_sem.at[0])
    wait(total_recv.at[pl.ds(0, ng - 1)], total_sem.at[0])


def hand_on(moments, residual, moments_out, residual_out, sems):
    copies = [
        pltpu.make_async_copy(moments, moments_out, sems.at[0]),
        pltpu.make_async_copy(residual, residual_out, sems.at[1]),
    ]
    for copy in copies:
        copy.start()
    for copy in copies:
        copy.wait()


def local(sizes, field, grain_positions, pixel_coords, block_grain, block_pixel, block_count):
    nx, nz, npl = sizes
    ng = nx * nz
    vmem = pl.BlockSpec(memory_space=pltpu.VMEM)
    moments, residual = pl.pallas_call(
        functools.partial(kernel, sizes),
        out_shape=(jax.ShapeDtypeStruct((3, 256), F32), jax.ShapeDtypeStruct((4, 128), F32)),
        in_specs=[pl.BlockSpec(memory_space=pltpu.HBM)] * 6,
        out_specs=(vmem, vmem),
        scratch_shapes=[
            pltpu.VMEM((4, 128), F32),
            pltpu.VMEM((3, 256), jnp.int32),
            pltpu.VMEM((3, ng * 512), jnp.int32),
            pltpu.VMEM((1, SLOTS), jnp.int32),
            pltpu.VMEM((1, SLOTS), jnp.int32),
            pltpu.VMEM((1, 1), jnp.int32),
            pltpu.VMEM((8, 128), jnp.int32),
            pltpu.SMEM((8, 128), jnp.int32),
            pltpu.VMEM((3, 4 * ng, 128), F32),
            pltpu.VMEM((SLOTS, 3, GROUPS, 2, 8, 128), F32),
            pltpu.VMEM((4, 3, GROUPS, 8, 128), F32),
            pltpu.VMEM((SLOTS, 24, 8, 128), F32),
            pltpu.VMEM((4 * ng, 384), jnp.bfloat16),
            pltpu.VMEM((3, 256, 128), F32),
            pltpu.VMEM((128, 128), F32),
            pltpu.VMEM((4 * ng, 128), F32),
            pltpu.VMEM((4 * ng, 128), F32),
            pltpu.VMEM((4 * ng, 128), F32),
            pltpu.VMEM((ITERS, 4, 128), F32),
            pltpu.VMEM((ITERS, ng, 4, 128), F32),
            pltpu.VMEM((ITERS, ng, 4, 128), F32),
            pltpu.VMEM((ITERS, ng - 1, 4, 128), F32),
            pltpu.VMEM((ITERS, 8, 128), F32),
            pltpu.VMEM((ITERS, npl, 8, 128), F32),
            pltpu.VMEM((1, 128), F32),
            pltpu.VMEM((npl, 1, 128), F32),
            pltpu.VMEM((1, 128), F32),
            pltpu.VMEM((ng, 1, 128), F32),
            pltpu.SemaphoreType.DMA((2, ITERS)),
            pltpu.SemaphoreType.DMA((2, ITERS)),
            pltpu.SemaphoreType.DMA((ITERS, 2)),
            pltpu.SemaphoreType.DMA((2,)),
            pltpu.SemaphoreType.DMA((2,)),
            pltpu.SemaphoreType.DMA((7,)),
        ],
        compiler_params=pltpu.CompilerParams(collective_id=1, has_side_effects=True, vmem_limit_bytes=40 << 20),
        name="solve",
    )(
        *(
            pltpu.with_memory_space_constraint(value, pltpu.HBM)
            for value in (field.reshape(4, 128), grain_positions, pixel_coords, block_grain, block_pixel)
        ),
        block_count,
    )
    held = pl.BlockSpec(memory_space=pltpu.HBM)
    moments, residual = pl.pallas_call(
        hand_on,
        out_shape=(jax.ShapeDtypeStruct((3, 256), F32), jax.ShapeDtypeStruct((4, 128), F32)),
        in_specs=[vmem] * 2,
        out_specs=(held, held),
        scratch_shapes=[pltpu.SemaphoreType.DMA((2,))],
        compiler_params=pltpu.CompilerParams(vmem_limit_bytes=40 << 20),
        name="hand_on",
    )(moments, residual)
    return moments, residual.reshape(512)


def solution(mesh, rows=4):
    grain, plane = mesh.shape["grain"], mesh.shape["plane"]
    placed = (
        P(("plane", "grain")),
        P(None, "grain"),
        P(None, "plane"),
        P("plane", "grain"),
        P("plane", "grain"),
        P("plane", "grain"),
    )
    return jax.shard_map(
        functools.partial(local, (rows, grain // rows, plane)),
        mesh=mesh,
        in_specs=placed,
        out_specs=(P(None, "grain"), P(("plane", "grain"))),
        check_vma=False,
    )
```
